128 devices in a mesh: lat: 8 (over z_lo, x), lon: 16 (over z_hi, y, core).
Axes of the slice: x: 4, y: 4, z: 4 (z_hi: 2, z_lo: 2; z = z_hi * 2 + z_lo), core: 2. Of those that a mesh axis runs over, the one named last changes fastest.
Arguments:
- fields: float32 [384, 768, 128], P('lat', 'lon'), may hold values from -6 to 6
- diffusion: float32 [128], replicated, may hold values from 0.3 to 30
- wave_slots: int32 [256], replicated, may hold values from 0 to 255, as said below
- reservoir_state: bfloat16 [192, 384, 4096], P('lat', 'lon'), may hold values from -0.8984375 to 0.8984375
- adjacency_blocks: bfloat16 [32, 8, 128, 128], replicated, may hold values from -0.1875 to 0.1875
- adjacency_index: int32 [32, 8], replicated, may hold values from 0 to 31, as said below
- input_index: int32 [4096], replicated, may hold values from 0 to 4607
- input_gain: float32 [4096], replicated, may hold values from -1.5 to 1.5
- bias: float32 [4096], replicated, may hold values from -0.5 to 0.5
- readout: bfloat16 [4096, 512], replicated, may hold values from -0.09375 to 0.09375
Outputs:
- blended_prediction: float32 [384, 768, 128], P('lat', 'lon')
- reservoir_next: bfloat16 [192, 384, 4096], P('lat', 'lon')
- spectral: float32 [256, 2, 256, 128], P(('lat', 'lon'))
The draws below stay inside these ranges and needn't reach their ends.
Inputs may be any that keep to these rules, and one draw needn't show every extreme that they name: `wave_slots`: a permutation of the wavenumbers in which slots 2 k and 2 k + 1 hold wavenumbers adding up to 255. `adjacency_index`: row g names block g and 7 other blocks, all different.
All inputs are finite; a program needn't handle non-finite values.
Results may differ from the reference program's by a relative error of at most 0.004.
The reference program's roundings to bfloat16 on the way count: a program that leaves them out, or rounds other values in their place, can miss the bound.
Values may be sent and summed in bfloat16 or wider, within the bound.
A program may use at most 256 MiB of HBM per device.

```python
import math
import jax
import jax.numpy as jnp
from jax import lax

PARALLEL_CIRCLES = 384
MERIDIAN_LINES = 768
WAVES = 256
STACKED_LAYERS = 128
RES = 4096
BLOCK = 128
CONN = 8
TILE = 2
HALO = 2
SPAN = 6


def draw_wave_slots(key, part):
    key = jax.random.fold_in(key, 11)
    first_key, second_key = jax.random.split(key)
    pairing = jax.random.permutation(first_key, WAVES // 2).astype(jnp.int32)
    flipped = jax.random.randint(second_key, (WAVES // 2,), 0, 2)
    partner = (WAVES - 1 - pairing).astype(jnp.int32)
    leading = jnp.where(flipped == 1, partner, pairing)
    trailing = jnp.where(flipped == 1, pairing, partner)
    return jnp.stack([leading, trailing], axis=1).reshape(WAVES).astype(jnp.int32)


def draw_adjacency_index(key, part):
    key = jax.random.fold_in(key, 23)
    block_count = RES // BLOCK
    subkeys = jax.random.split(key, block_count)

    def pick_offsets(subkey):
        return jax.random.permutation(subkey, block_count - 1)[:CONN - 1].astype(jnp.int32) + 1
    offsets = jax.vmap(pick_offsets)(subkeys)
    row_ids = jnp.arange(block_count, dtype=jnp.int32)[:, None]
    chosen = jnp.concatenate([row_ids, (row_ids + offsets) % block_count], axis=1)
    return chosen.astype(jnp.int32)


def place_ends(result, rng, least, top_value):
    index_at = [jax.random.randint(jax.random.fold_in(rng, axis), (), 0, length) for axis, length in enumerate(result.shape)]
    widest = result.shape.index(max(result.shape))
    beside = index_at[:widest] + [(index_at[widest] + 1) % result.shape[widest]] + index_at[widest + 1:]
    return result.at[tuple(index_at)].set(least).at[tuple(beside)].set(top_value)


def block_levels(key, shape, shards, low, high):
    def one(axis_at, parts):
        steps = jax.random.uniform(jax.random.fold_in(jax.random.fold_in(key, 6), axis_at), (parts,), jnp.float32, low / len(shards), high / len(shards))
        return jnp.repeat(jnp.exp(steps), shape[axis_at] // parts).reshape((-1,) + (1,) * (len(shape) - axis_at - 1))

    factor_of = one(*shards[0])
    for cut in shards[1:]:
        factor_of = factor_of * one(*cut)
    return factor_of


def centred(key, extent, scale, most, shards=(), kind=jnp.bfloat16):
    result = jax.random.normal(key, extent, jnp.float32) * scale
    if len(shards) > 0:
        result = block_levels(key, extent, shards, -0.22, 0.18) * result
    return jnp.clip(result, min=-most, max=most).astype(kind)


def setup_inputs(seed: int = 0) -> dict:
    key_of = jax.random.split(jax.random.key(seed), 11)
    return {
        "fields": centred(key_of[0], (PARALLEL_CIRCLES, MERIDIAN_LINES, STACKED_LAYERS), 1.0, 6.0, ((0, 8), (1, 16)), jnp.float32),
        "diffusion": jnp.clip(jnp.exp(jax.random.uniform(key_of[1], (STACKED_LAYERS,), jnp.float32, math.log(0.3), math.log(30.0))), 0.3, 30.0),
        "wave_slots": draw_wave_slots(jax.random.fold_in(key_of[10], 71), 0),
        "reservoir_state": jnp.clip(jax.random.uniform(key_of[3], (PARALLEL_CIRCLES // TILE, MERIDIAN_LINES // TILE, RES), jnp.float32, -0.8984375, 0.8984375) * block_levels(key_of[3], (PARALLEL_CIRCLES // TILE, MERIDIAN_LINES // TILE, RES), ((0, 8), (1, 16)), -0.4, 0.0), -0.8984375, 0.8984375).astype(jnp.bfloat16),
        "adjacency_blocks": centred(key_of[4], (RES // BLOCK, CONN, BLOCK, BLOCK), (CONN * BLOCK) ** -0.5, 0.1875),
        "adjacency_index": draw_adjacency_index(jax.random.fold_in(key_of[10], 71), 0),
        "input_index": place_ends(jax.random.randint(key_of[6], (RES,), 0, SPAN * SPAN * STACKED_LAYERS), jax.random.fold_in(key_of[6], 1), 0, (SPAN * SPAN * STACKED_LAYERS) - 1).astype(jnp.int32),
        "input_gain": jnp.clip(jax.random.uniform(key_of[7], (RES,), jnp.float32, -1.5, 1.5), -1.5, 1.5),
        "bias": jnp.clip(jax.random.uniform(key_of[8], (RES,), jnp.float32, -0.5, 0.5), -0.5, 0.5),
        "readout": centred(key_of[9], (RES, TILE * TILE * STACKED_LAYERS), RES ** -0.5, 0.09375),
    }


def grid_geometry():
    colatitude = (jnp.arange(PARALLEL_CIRCLES).astype(jnp.float32) + 0.5) * (math.pi / PARALLEL_CIRCLES)
    cos_col = jnp.cos(colatitude)
    sin_col = jnp.sin(colatitude)
    return (cos_col, jnp.log(sin_col), math.pi / PARALLEL_CIRCLES * sin_col)

def damping_table(diffusion):
    degree = jnp.arange(WAVES).astype(jnp.float32)
    scaled = degree * (degree + 1.0) / float((WAVES - 1) * WAVES)
    return 1.0 / (1.0 + diffusion[None, :] * (scaled * scaled)[:, None])

def degree_start(wave_ints, log_sin):
    halves = jnp.arange(1, WAVES).astype(jnp.float32)
    partial_logs = jnp.concatenate([jnp.zeros((1,), jnp.float32), jnp.cumsum(jnp.log1p(0.5 / halves))])
    chosen = partial_logs[wave_ints]
    orders = wave_ints.astype(jnp.float32)
    return jnp.exp(0.5 * chosen[:, None] + orders[:, None] * log_sin[None, :] - 0.5 * math.log(2.0))

def legendre_table(wave_ints, cos_col, log_sin):
    orders = wave_ints.astype(jnp.float32)[:, None]
    pole_value = degree_start(wave_ints, log_sin)
    order_sq = orders * orders

    def one_degree(previous, current, degree):
        level = degree.astype(jnp.float32)
        above = level > orders
        prior = level - 1.0
        coef_a = jnp.sqrt(jnp.where(above, 4.0 * level * level - 1.0, 1.0) / jnp.where(above, level * level - order_sq, 1.0))
        coef_b = jnp.sqrt(jnp.where(above, prior * prior - order_sq, 0.0) / jnp.where(level > 1.5, 4.0 * prior * prior - 1.0, 1.0))
        return jnp.where(above, coef_a * (cos_col[None, :] * current - coef_b * previous), jnp.where(level == orders, pole_value, 0.0))

    def block_step(last_pair, block_base):
        previous, current = last_pair
        stacked = []
        for offset in range(16):
            degree_row = one_degree(previous, current, block_base * 16 + offset)
            previous, current = (current, degree_row)
            stacked.append(degree_row)
        return ((previous, current), jnp.stack(stacked))
    empty_rows = jnp.zeros(pole_value.shape, jnp.float32)
    last_pair, blocks = lax.scan(block_step, (empty_rows, empty_rows), jnp.arange(WAVES // 16, dtype=jnp.int32))
    return jnp.transpose(blocks.reshape(WAVES, pole_value.shape[0], pole_value.shape[1]), (1, 0, 2))

def reference(fields, diffusion, wave_slots, reservoir_state, adjacency_blocks, adjacency_index, input_index, input_gain, bias, readout):
    cos_col, log_sin, weights = grid_geometry()
    damping = damping_table(diffusion)
    spectrum = jnp.fft.rfft(fields, axis=1)[:, :WAVES, :] / MERIDIAN_LINES
    zonal = jnp.stack([jnp.real(spectrum), jnp.imag(spectrum)], axis=0)

    def wave_group(group):
        first_wave = group * 16
        wave_ints = (jnp.arange(16, dtype=jnp.int32) + first_wave).astype(jnp.int32)
        table = legendre_table(wave_ints, cos_col, log_sin)
        portion = lax.dynamic_slice_in_dim(zonal, first_wave, 16, 2)
        coefficients = jnp.einsum('snj,pjsc->spnc', table * weights[None, None, :], portion, precision=lax.Precision.HIGHEST)
        filtered = coefficients * damping[None, None, :, :]
        grid_part = jnp.einsum('snj,spnc->pjsc', table, filtered, precision=lax.Precision.HIGHEST)
        return (filtered, grid_part)
    filtered, grid_part = lax.map(wave_group, jnp.arange(WAVES // 16, dtype=jnp.int32))
    filtered = filtered.reshape(WAVES, 2, WAVES, STACKED_LAYERS)
    spectral = filtered[wave_slots]
    grid_zonal = jnp.transpose(grid_part, (1, 2, 0, 3, 4)).reshape(2, PARALLEL_CIRCLES, WAVES, STACKED_LAYERS)
    fourier_mode_amplitudes = lax.complex(grid_zonal[0], grid_zonal[1])
    fourier_mode_amplitudes = jnp.pad(fourier_mode_amplitudes, ((0, 0), (0, MERIDIAN_LINES // 2 + 1 - WAVES), (0, 0)))
    predicted_state = jnp.fft.irfft(fourier_mode_amplitudes, n=MERIDIAN_LINES, axis=1) * MERIDIAN_LINES
    physics_model_state = predicted_state.astype(jnp.bfloat16)
    framed = jnp.pad(physics_model_state, ((HALO, HALO), (0, 0), (0, 0)))
    framed = jnp.concatenate([framed[:, MERIDIAN_LINES - HALO:], framed, framed[:, :HALO]], axis=1)
    window = TILE + 2 * HALO
    lat_offset = input_index // (window * STACKED_LAYERS)
    lon_offset = input_index // STACKED_LAYERS % window
    channel = input_index % STACKED_LAYERS
    tile_cols = MERIDIAN_LINES // TILE
    col_index = TILE * jnp.arange(tile_cols, dtype=jnp.int32)[:, None] + lon_offset[None, :]
    block_count = RES // BLOCK

    def tile_row(row_id):
        strip = lax.dynamic_slice_in_dim(framed, row_id * TILE, window, 0)
        picked = strip[lat_offset[None, :], col_index, channel[None, :]]
        drive = picked.astype(jnp.float32) * input_gain[None, :]
        states = reservoir_state[row_id].reshape(tile_cols, block_count, BLOCK)
        linked = jnp.take(states, adjacency_index, axis=1).astype(jnp.float32)
        recur = jnp.einsum('tikq,ikpq->tip', linked, adjacency_blocks.astype(jnp.float32))
        upcoming = jnp.tanh(recur.reshape(tile_cols, RES) + drive + bias[None, :]).astype(jnp.bfloat16)
        trained_residual_adjustment = jnp.dot(upcoming, readout, preferred_element_type=jnp.float32)
        trained_residual_adjustment = trained_residual_adjustment.reshape(tile_cols, TILE, TILE, STACKED_LAYERS).transpose(1, 0, 2, 3).reshape(TILE, MERIDIAN_LINES, STACKED_LAYERS)
        return (upcoming, trained_residual_adjustment)
    reservoir_next, trained_residual_adjustment = lax.map(tile_row, jnp.arange(PARALLEL_CIRCLES // TILE, dtype=jnp.int32))
    blended_prediction = predicted_state + trained_residual_adjustment.reshape(PARALLEL_CIRCLES, MERIDIAN_LINES, STACKED_LAYERS)
    return (blended_prediction, reservoir_next, spectral)
```

```python
import functools
import math

import jax
import jax.numpy as jnp
import numpy as np
from jax import lax
from jax.experimental import pallas as pl
from jax.experimental.pallas import tpu as pltpu
from jax.sharding import PartitionSpec as P

ROWS = 384
COLS = 768
WAVES = 256
CHANNELS = 128
RES = 4096
BLOCK = 128
CONN = 8
TILE = 2
WINDOW = 6
LATS = 8
LONS = 16
DEVICES = LATS * LONS
SUB_ROWS = ROWS // DEVICES
BAND = 48
HALF = 28
SENT_COLS = 2 * HALF
TILES = 24
FRAME = TILES + 2
CHUNK = 512
CHUNKS = RES // CHUNK
PICK = 2 * WINDOW * CHANNELS
MB = 1 << 20


def geometry():
    j = np.arange(ROWS).reshape(DEVICES, SUB_ROWS).T.reshape(-1)
    colatitude = (j + 0.5) * (math.pi / ROWS)
    return np.cos(colatitude), np.sin(colatitude)


def order_rows():
    m = np.arange(WAVES)[:, None].astype(np.float64)
    n = np.arange(WAVES)[None, :].astype(np.float64)
    above = n > m
    above_sq = np.where(above, 4 * n * n - 1, 0.0)
    a = np.sqrt(above_sq / np.where(above, n * n - m * m, 1.0))
    b = np.sqrt(
        np.where(above, (n - 1) ** 2 - m * m, 0.0) / np.where(n > 1.5, 4 * (n - 1) ** 2 - 1, 1.0)
    )
    e = (n == m).astype(np.float64)
    factors = np.concatenate([a, a * b, e], axis=1)
    _, sin_col = geometry()
    halves = np.arange(1, WAVES)
    logs = np.concatenate([[0.0], np.cumsum(np.log1p(0.5 / halves))])
    pole = np.exp(0.5 * logs[:, None] + m * np.log(sin_col)[None, :] - 0.5 * math.log(2.0))
    return factors.astype(np.float32), pole.astype(np.float32)


def forward_rows():
    m = np.arange(WAVES)[:, None]
    k = np.arange(COLS)[None, :]
    angle = (m * k % COLS) * (2.0 * math.pi / COLS)
    table = np.stack([np.cos(angle), -np.sin(angle)], axis=1) / COLS
    return table.reshape(2 * WAVES, COLS)


def inverse_columns():
    o = np.arange(LONS)[:, None, None]
    b = np.arange(2)[None, :, None]
    t = np.arange(HALF)[None, None, :]
    k = ((BAND * o - 2 + 2 * t + b) % COLS).reshape(-1)
    m = np.arange(WAVES)[None, :]
    angle = (m * k[:, None] % COLS) * (2.0 * math.pi / COLS)
    factor = np.where(m == 0, 1.0, 2.0)
    table = np.stack([factor * np.cos(angle), -factor * np.sin(angle)], axis=2)
    return table.reshape(LONS * SENT_COLS, 2 * WAVES)


def legendre_kernel(factor_ref, pole_ref, cos_ref, weight_ref, table_ref, weighted_ref, rows_ref):
    cos_col = cos_ref[...]
    poles = [pole_ref[pl.ds(s, 1), :] for s in range(2)]

    def eight(base, carry):
        state = list(carry)
        stacked = [[], []]
        for step in range(8):
            n = base * 8 + step
            for s in range(2):
                previous, current = state[s]
                a = factor_ref[s, n]
                ab = factor_ref[s, WAVES + n]
                e = factor_ref[s, 2 * WAVES + n]
                value = a * (cos_col * current) - ab * previous + e * poles[s]
                state[s] = (current, value)
                stacked[s].append(value)
        for s in range(2):
            rows_ref[s, pl.ds(pl.multiple_of(base * 8, 8), 8), :] = jnp.concatenate(
                stacked[s], axis=0
            )
        return tuple(state)

    zero = jnp.zeros((1, ROWS), jnp.float32)
    lax.fori_loop(0, WAVES // 8, eight, ((zero, zero), (zero, zero)))
    for s in range(2):
        rows = rows_ref[s]
        table_ref[s] = rows.astype(jnp.bfloat16)
        weighted_ref[s] = (rows * weight_ref[...]).astype(jnp.bfloat16)


def dft_kernel(table_ref, rows_ref, out_ref):
    data = rows_ref[...]
    whole = jnp.concatenate(
        [data[:, r].reshape(COLS, CHANNELS) for r in range(SUB_ROWS)], axis=1
    )
    out_ref[...] = jnp.dot(
        table_ref[...], whole, preferred_element_type=jnp.float32
    ).astype(jnp.bfloat16)


def spectral_kernel(
    owned_ref, weighted_ref, table_ref, diffusion_ref, spectral_ref, grid_ref, wide_ref, back_ref
):
    for r in range(SUB_ROWS):
        wide_ref[r] = owned_ref[:, r * 128 : (r + 1) * 128].astype(jnp.float32)
    degree = lax.broadcasted_iota(jnp.int32, (WAVES, CHANNELS), 0).astype(jnp.float32)
    scaled = degree * (degree + 1.0) / float((WAVES - 1) * WAVES)
    damping = 1.0 / (1.0 + diffusion_ref[...] * (scaled * scaled))
    damping = jnp.concatenate([damping, damping], axis=1)
    for s in range(2):
        parts = []
        for p in range(2):
            parts.append(
                jnp.concatenate(
                    [
                        wide_ref[r, pl.ds(2 * s + p, DEVICES, stride=4), :]
                        for r in range(SUB_ROWS)
                    ],
                    axis=0,
                )
            )
        zonal = jnp.concatenate(parts, axis=1).astype(jnp.bfloat16)
        filtered = damping * jnp.dot(
            weighted_ref[s], zonal, preferred_element_type=jnp.float32
        )
        for p in range(2):
            spectral_ref[s, p] = filtered[:, p * 128 : (p + 1) * 128]
        grid = lax.dot_general(
            table_ref[s],
            filtered.astype(jnp.bfloat16),
            (((0,), (0,)), ((), ())),
            preferred_element_type=jnp.float32,
        )
        for p in range(2):
            for r in range(SUB_ROWS):
                back_ref[r, pl.ds(2 * s + p, DEVICES, stride=4), :] = grid[
                    r * 128 : (r + 1) * 128, p * 128 : (p + 1) * 128
                ]
    for r in range(SUB_ROWS):
        grid_ref[:, r * 128 : (r + 1) * 128] = back_ref[r].astype(jnp.bfloat16)


def recur_kernel(index_ref, state_ref, blocks_ref, key_ref, recur_ref, pick_ref):
    chunk = pl.program_id(0)
    per = CHUNK // BLOCK
    for g in range(per):
        columns = []
        for l in range(CONN):
            at = index_ref[chunk * per + g, l]
            columns.append(state_ref[:, pl.ds(pl.multiple_of(at * BLOCK, BLOCK), BLOCK)])
        left = jnp.concatenate(columns, axis=1)
        right = jnp.concatenate([blocks_ref[g, l] for l in range(CONN)], axis=1)
        recur_ref[:, g * BLOCK : (g + 1) * BLOCK] = lax.dot_general(
            left, right, (((1,), (1,)), ((), ())), preferred_element_type=jnp.float32
        )
    entry = lax.broadcasted_iota(jnp.int32, (PICK, CHUNK), 0)
    pick_ref[...] = jnp.where(entry == key_ref[...], 1.0, 0.0).astype(jnp.bfloat16)


def reservoir_kernel(
    rows_ref,
    low_ref,
    high_ref,
    pick_ref,
    recur_ref,
    node_ref,
    gain_ref,
    readout_ref,
    blend_ref,
    next_ref,
    frame_ref,
    drive_ref,
    total_ref,
):
    chunk = pl.program_id(0)

    @pl.when(chunk == 0)
    def _():
        def row_of(position):
            if position < 2:
                part = low_ref[:, position * 128 : (position + 1) * 128]
            elif position >= BAND + 2:
                at = position - BAND - 2
                part = high_ref[:, at * 128 : (at + 1) * 128]
            else:
                j = position - 2
                at = j % SUB_ROWS
                part = rows_ref[j // SUB_ROWS, :, at * 128 : (at + 1) * 128]
            return part.astype(jnp.float32)

        for pair in range(FRAME // 2):
            for a in range(2):
                upper = row_of(4 * pair + a)
                lower = row_of(4 * pair + 2 + a)
                for b in range(WINDOW):
                    start = (b % 2) * HALF + b // 2
                    both = jnp.concatenate(
                        [upper[start : start + TILES], lower[start : start + TILES]], axis=0
                    )
                    at = (b * 2 + a) * 128
                    frame_ref[pair * 48 : (pair + 1) * 48, at : at + 128] = both.astype(
                        jnp.bfloat16
                    )
        total_ref[...] = jnp.zeros_like(total_ref)

    drive_ref[...] = jnp.dot(frame_ref[...], pick_ref[...], preferred_element_type=jnp.float32)
    count = TILES * TILES
    row = node_ref[...]
    picked = jnp.where(
        row == 0,
        drive_ref[0:count],
        jnp.where(row == 1, drive_ref[TILES : count + TILES], drive_ref[2 * TILES :]),
    )
    upcoming = jnp.tanh(recur_ref[...] + picked * gain_ref[0:1, :] + gain_ref[1:2, :]).astype(
        jnp.bfloat16
    )
    next_ref[...] = upcoming
    total_ref[...] += jnp.dot(upcoming, readout_ref[...], preferred_element_type=jnp.float32)

    @pl.when(chunk == CHUNKS - 1)
    def _():
        for a in range(2):
            for b in range(2):
                at = ((2 + b) * 2 + a) * 128
                forecast = frame_ref[:, at : at + 128].astype(jnp.float32)
                to = (a * 2 + b) * 128
                for i in range(TILES):
                    blend_ref[pl.ds((2 * i + a) * BAND + b, TILES, stride=2), :] = (
                        forecast[(i + 1) * TILES : (i + 2) * TILES]
                        + total_ref[i * TILES : (i + 1) * TILES, to : to + 128]
                    )


def shards(
    fields,
    diffusion,
    wave_slots,
    reservoir_state,
    adjacency_blocks,
    adjacency_index,
    input_index,
    input_gain,
    bias,
    readout,
):
    vmem = pl.BlockSpec(memory_space=pltpu.VMEM)
    smem = pl.BlockSpec(memory_space=pltpu.SMEM)
    lat = lax.axis_index("lat")
    owner = lat * LONS + lax.axis_index("lon")

    sent = fields.reshape(LONS, SUB_ROWS * BAND, CHANNELS).astype(jnp.bfloat16)
    row_data = lax.all_to_all(sent, "lon", split_axis=0, concat_axis=0, tiled=True)

    slot_part = (2 * wave_slots[:, None] + jnp.arange(2, dtype=jnp.int32)).reshape(-1)
    chosen = (
        slot_part[:, None] == jnp.arange(2 * WAVES, dtype=jnp.int32)[None, :]
    ).astype(jnp.bfloat16)
    forward = jnp.dot(chosen, jnp.asarray(forward_rows(), jnp.bfloat16)).astype(jnp.bfloat16)
    inverse = lax.dot_general(
        jnp.asarray(inverse_columns(), jnp.bfloat16), chosen, (((1,), (1,)), ((), ()))
    ).astype(jnp.bfloat16)
    factors, poles = order_rows()
    factors, poles = jnp.asarray(factors), jnp.asarray(poles)
    owned = lax.dynamic_slice_in_dim(wave_slots, owner * 2, 2)
    own_factors = jnp.concatenate(
        [lax.dynamic_slice_in_dim(factors, owned[s], 1) for s in range(2)], axis=0
    )
    own_poles = jnp.concatenate(
        [lax.dynamic_slice_in_dim(poles, owned[s], 1) for s in range(2)], axis=0
    )
    cos_col, sin_col = geometry()
    table_shape = jax.ShapeDtypeStruct((2, WAVES, ROWS), jnp.bfloat16)
    table, weighted = pl.pallas_call(
        legendre_kernel,
        out_shape=(table_shape, table_shape),
        in_specs=[smem, vmem, vmem, vmem],
        out_specs=(vmem, vmem),
        scratch_shapes=[pltpu.VMEM((2, WAVES, ROWS), jnp.float32)],
        cost_estimate=pl.CostEstimate(flops=2000000, bytes_accessed=800000, transcendentals=0),
        name="legendre",
    )(
        own_factors,
        own_poles,
        jnp.asarray(cos_col[None, :], jnp.float32),
        jnp.asarray((math.pi / ROWS) * sin_col[None, :], jnp.float32),
    )

    states = reservoir_state.reshape(TILES * TILES, RES)
    row_at = input_index // (WINDOW * CHANNELS)
    col_at = input_index // CHANNELS % WINDOW
    key = (col_at * 2 + row_at % 2) * CHANNELS + input_index % CHANNELS
    recur, pick = pl.pallas_call(
        recur_kernel,
        grid=(CHUNKS,),
        out_shape=(
            jax.ShapeDtypeStruct((TILES * TILES, RES), jnp.float32),
            jax.ShapeDtypeStruct((PICK, RES), jnp.bfloat16),
        ),
        in_specs=[
            smem,
            pl.BlockSpec((TILES * TILES, RES), lambda c: (0, 0)),
            pl.BlockSpec((CHUNK // BLOCK, CONN, BLOCK, BLOCK), lambda c: (c, 0, 0, 0)),
            pl.BlockSpec((1, CHUNK), lambda c: (0, c)),
        ],
        out_specs=(
            pl.BlockSpec((TILES * TILES, CHUNK), lambda c: (0, c)),
            pl.BlockSpec((PICK, CHUNK), lambda c: (0, c)),
        ),
        compiler_params=pltpu.CompilerParams(vmem_limit_bytes=32 * MB),
        cost_estimate=pl.CostEstimate(
            flops=2 * TILES * TILES * RES * CONN * BLOCK,
            bytes_accessed=36 * MB,
            transcendentals=0,
        ),
        name="recur",
    )(adjacency_index, states, adjacency_blocks, key[None, :])

    zonal = pl.pallas_call(
        dft_kernel,
        out_shape=jax.ShapeDtypeStruct((2 * WAVES, SUB_ROWS * CHANNELS), jnp.bfloat16),
        in_specs=[vmem, vmem],
        out_specs=vmem,
        name="dft",
    )(forward, row_data.reshape(LONS, SUB_ROWS, BAND, CHANNELS))
    owned_coef = lax.all_to_all(
        zonal.reshape(DEVICES, 4, SUB_ROWS * CHANNELS),
        ("lat", "lon"),
        split_axis=0,
        concat_axis=0,
        tiled=True,
    )
    spectral, grid_part = pl.pallas_call(
        spectral_kernel,
        out_shape=(
            jax.ShapeDtypeStruct((2, 2, WAVES, CHANNELS), jnp.float32),
            jax.ShapeDtypeStruct((4 * DEVICES, SUB_ROWS * CHANNELS), jnp.bfloat16),
        ),
        in_specs=[vmem, vmem, vmem, vmem],
        out_specs=(vmem, vmem),
        scratch_shapes=[
            pltpu.VMEM((SUB_ROWS, 4 * DEVICES, CHANNELS), jnp.float32),
            pltpu.VMEM((SUB_ROWS, 4 * DEVICES, CHANNELS), jnp.float32),
        ],
        name="spectral",
    )(
        owned_coef.reshape(4 * DEVICES, SUB_ROWS * CHANNELS),
        weighted,
        table,
        diffusion[None, :],
    )
    back = lax.all_to_all(
        grid_part.reshape(DEVICES, 4, SUB_ROWS * CHANNELS),
        ("lat", "lon"),
        split_axis=0,
        concat_axis=0,
        tiled=True,
    )
    samples = jnp.dot(
        inverse,
        back.reshape(4 * DEVICES, SUB_ROWS * CHANNELS),
        preferred_element_type=jnp.float32,
    ).astype(jnp.bfloat16)
    framed = lax.all_to_all(
        samples.reshape(LONS, SENT_COLS, SUB_ROWS * CHANNELS),
        "lon",
        split_axis=0,
        concat_axis=0,
        tiled=True,
    )
    up = [(i, i + 1) for i in range(LATS - 1)]
    down = [(i + 1, i) for i in range(LATS - 1)]
    low = lax.ppermute(framed[LONS - 1, :, CHANNELS:], "lat", up)
    high = lax.ppermute(framed[0, :, : 2 * CHANNELS], "lat", down)

    const = lambda *zeros: (lambda c: zeros)
    blended, upcoming = pl.pallas_call(
        reservoir_kernel,
        grid=(CHUNKS,),
        out_shape=(
            jax.ShapeDtypeStruct((BAND * BAND, CHANNELS), jnp.float32),
            jax.ShapeDtypeStruct((TILES * TILES, RES), jnp.bfloat16),
        ),
        in_specs=[
            pl.BlockSpec((LONS, SENT_COLS, SUB_ROWS * CHANNELS), const(0, 0, 0)),
            pl.BlockSpec((SENT_COLS, 2 * CHANNELS), const(0, 0)),
            pl.BlockSpec((SENT_COLS, 2 * CHANNELS), const(0, 0)),
            pl.BlockSpec((PICK, CHUNK), lambda c: (0, c)),
            pl.BlockSpec((TILES * TILES, CHUNK), lambda c: (0, c)),
            pl.BlockSpec((1, CHUNK), lambda c: (0, c)),
            pl.BlockSpec((2, CHUNK), lambda c: (0, c)),
            pl.BlockSpec((CHUNK, 4 * CHANNELS), lambda c: (c, 0)),
        ],
        out_specs=(
            pl.BlockSpec((BAND * BAND, CHANNELS), const(0, 0)),
            pl.BlockSpec((TILES * TILES, CHUNK), lambda c: (0, c)),
        ),
        scratch_shapes=[
            pltpu.VMEM((FRAME * TILES, PICK), jnp.bfloat16),
            pltpu.VMEM((FRAME * TILES, CHUNK), jnp.float32),
            pltpu.VMEM((TILES * TILES, 4 * CHANNELS), jnp.float32),
        ],
        compiler_params=pltpu.CompilerParams(vmem_limit_bytes=32 * MB),
        cost_estimate=pl.CostEstimate(
            flops=2 * FRAME * TILES * RES * PICK,
            bytes_accessed=36 * MB,
            transcendentals=TILES * TILES * RES,
        ),
        name="reservoir",
    )(
        framed,
        low,
        high,
        pick,
        recur,
        (row_at // 2)[None, :],
        jnp.stack([input_gain, bias]),
        readout,
    )
    return (
        blended.reshape(BAND, BAND, CHANNELS),
        upcoming.reshape(TILES, TILES, RES),
        spectral,
    )


def solution(mesh):
    placed = (P("lat", "lon", None), P(), P(), P("lat", "lon", None), P(), P(), P(), P(), P(), P())
    return jax.shard_map(
        shards,
        mesh=mesh,
        in_specs=placed,
        out_specs=(
            P("lat", "lon", None),
            P("lat", "lon", None),
            P(("lat", "lon"), None, None, None),
        ),
        check_vma=False,
    )
```

```python
import functools
import math

import jax
import jax.numpy as jnp
import numpy as np
from jax import lax
from jax.experimental import pallas as pl
from jax.experimental.pallas import tpu as pltpu
from jax.sharding import PartitionSpec as P

ROWS = 384
COLS = 768
WAVES = 256
CHANNELS = 128
RES = 4096
BLOCK = 128
CONN = 8
TILE = 2
WINDOW = 6
LATS = 8
LONS = 16
DEVICES = LATS * LONS
CHIPS = DEVICES // 2
SUB_ROWS = ROWS // DEVICES
BAND = 48
HALF = 28
SENT_COLS = 2 * HALF
TILES = 24
FRAME = TILES + 2
CHUNK = 512
CHUNKS = RES // CHUNK
PICK = 2 * WINDOW * CHANNELS
MB = 1 << 20
MESH = pl.DeviceIdType.MESH
SPLIT = (7, 16, 24, 32)
LANES = SUB_ROWS * CHANNELS
NODES = TILES * TILES


def geometry():
    j = np.arange(ROWS).reshape(CHIPS, 2, SUB_ROWS).transpose(2, 1, 0).reshape(-1)
    colatitude = (j + 0.5) * (math.pi / ROWS)
    return np.cos(colatitude), np.sin(colatitude)


def log_terms():
    index = np.arange(WAVES).astype(np.float64)
    return np.where(index > 0, np.log1p(0.5 / np.maximum(index, 1.0)), 0.0)


def forward_rows():
    m = np.arange(WAVES)[:, None]
    k = np.arange(COLS)[None, :]
    angle = (m * k % COLS) * (2.0 * math.pi / COLS)
    table = np.stack([np.cos(angle), -np.sin(angle)], axis=1) / COLS
    return table.reshape(2 * WAVES, COLS)


def inverse_columns():
    o = np.arange(LONS)[:, None, None]
    b = np.arange(2)[None, :, None]
    t = np.arange(HALF)[None, None, :]
    k = ((BAND * o - 2 + 2 * t + b) % COLS).reshape(-1)
    m = np.arange(WAVES)[None, :]
    angle = (m * k[:, None] % COLS) * (2.0 * math.pi / COLS)
    factor = np.where(m == 0, 1.0, 2.0)
    table = np.stack([factor * np.cos(angle), -factor * np.sin(angle)], axis=2)
    return table.reshape(LONS * SENT_COLS, 2 * WAVES)


def split(table):
    high = table.astype(jnp.bfloat16)
    return high, (table - high.astype(np.float32)).astype(jnp.bfloat16)


def chain_kernel(
    slots_ref,
    index_ref,
    fields_ref,
    column_ref,
    row_ref,
    forward_high_ref,
    forward_low_ref,
    inverse_ref,
    cos_ref,
    log_sin_ref,
    weight_ref,
    diffusion_ref,
    logs_ref,
    states_hbm,
    blocks_hbm,
    spectral_ref,
    framed_ref,
    halo_ref,
    recur_hbm,
    states_ref,
    blocks_ref,
    recur_ref,
    sent_ref,
    rows_ref,
    table_ref,
    factor_ref,
    legendre_ref,
    weighted_ref,
    plain_ref,
    zonal_ref,
    sibling_ref,
    message_ref,
    owned_ref,
    wide_ref,
    back_ref,
    reply_ref,
    replied_ref,
    mine_ref,
    other_ref,
    inverted_ref,
    samples_ref,
    load_sem,
    store_sem,
    lon_send,
    lon_recv,
    core_send,
    core_recv,
    out_send,
    out_recv,
    back_send,
    back_recv,
    grid_send,
    grid_recv,
    halo_send,
    halo_recv,
):
    a = lax.axis_index("lat")
    o = lax.axis_index("lon")
    core = lax.rem(o, 2)
    chip = a * (LONS // 2) + lax.div(o, 2)
    sibling = (a, o + 1 - 2 * core)

    def lon_at(step):
        return lax.rem(o + step, LONS)

    def chip_at(step):
        return lax.rem(chip + step, CHIPS)

    def chip_device(step):
        other = chip_at(step)
        return (lax.div(other, LONS // 2), 2 * lax.rem(other, LONS // 2) + core)

    def each(count, action):
        def step(s, carry):
            action(s)
            return carry

        lax.fori_loop(1, count, step, 0)

    def load_states(b):
        return pltpu.make_async_copy(
            states_hbm.at[:, pl.ds(pl.multiple_of(b * BLOCK, BLOCK), BLOCK)],
            states_ref.at[b],
            load_sem.at[b],
        )

    load_blocks = pltpu.make_async_copy(blocks_hbm, blocks_ref, load_sem.at[RES // BLOCK])

    barrier = pltpu.get_barrier_semaphore()
    each(
        LONS,
        lambda s: pl.semaphore_signal(
            barrier, inc=1, device_id=(a, lon_at(s)), device_id_type=MESH
        ),
    )
    each(
        CHIPS,
        lambda s: pl.semaphore_signal(
            barrier, inc=1, device_id=chip_device(s), device_id_type=MESH
        ),
    )
    load_blocks.start()
    each(RES // BLOCK, lambda b: load_states(b).start())
    load_states(0).start()
    halo_ref[...] = jnp.zeros_like(halo_ref)
    for d in range(LONS):
        sent_ref[d] = fields_ref[d * 144 : (d + 1) * 144, :].astype(jnp.bfloat16)
    pl.semaphore_wait(barrier, LONS + CHIPS - 2)

    def row_copy(s):
        return pltpu.make_async_remote_copy(
            src_ref=sent_ref.at[lon_at(s)],
            dst_ref=rows_ref.at[o],
            send_sem=lon_send.at[s],
            recv_sem=lon_recv.at[s],
            device_id=(a, lon_at(s)),
            device_id_type=MESH,
        )

    each(LONS, lambda s: row_copy(s).start())
    rows_ref[o] = sent_ref[o]

    entry = lax.broadcasted_iota(jnp.int32, (2 * WAVES, 2 * WAVES), 1)
    chosen = jnp.where(entry == column_ref[...], 1.0, 0.0).astype(jnp.bfloat16)
    for half, source in enumerate((forward_high_ref, forward_low_ref)):
        table_ref[half] = jnp.dot(
            chosen, source[...], preferred_element_type=jnp.float32
        ).astype(jnp.bfloat16)

    level = lax.broadcasted_iota(jnp.int32, (WAVES, CHANNELS), 0).astype(jnp.float32)
    cos_col = cos_ref[...]
    poles = []
    for s in range(2):
        m = slots_ref[2 * (a * LONS + o) + s]
        order = m.astype(jnp.float32)
        above = level > order
        order_sq = order * order
        prior = level - 1.0
        factor = jnp.sqrt(
            jnp.where(above, 4.0 * level * level - 1.0, 0.0)
            / jnp.where(above, level * level - order_sq, 1.0)
        )
        factor_ref[s, 0] = factor
        factor_ref[s, 1] = factor * jnp.sqrt(
            jnp.where(above, prior * prior - order_sq, 0.0)
            / jnp.where(level > 1.5, 4.0 * prior * prior - 1.0, 1.0)
        )
        factor_ref[s, 2] = jnp.where(level == order, 1.0, 0.0)
        index = lax.broadcasted_iota(jnp.int32, (1, WAVES), 1)
        logs = jnp.sum(jnp.where(index <= m, logs_ref[...], 0.0), axis=1, keepdims=True)
        poles.append(
            jnp.exp(0.5 * logs + order * log_sin_ref[...] - 0.5 * math.log(2.0))
        )

    def eight(base, carry):
        state = list(carry)
        at = pl.ds(pl.multiple_of(base * 8, 8), 8)
        for s in range(2):
            previous, current = state[s]
            factors = [factor_ref[s, f, at, :] for f in range(3)]
            stacked = []
            for step in range(8):
                row, drop, first = [
                    jnp.concatenate([f[step : step + 1]] * SUB_ROWS, axis=1) for f in factors
                ]
                value = row * (cos_col * current) - drop * previous + first * poles[s]
                previous, current = current, value
                stacked.append(value)
            state[s] = (previous, current)
            legendre_ref[s, at, :] = jnp.concatenate(stacked, axis=0)
        return tuple(state)

    zero = jnp.zeros((1, ROWS), jnp.float32)
    lax.fori_loop(0, WAVES // 8, eight, ((zero, zero), (zero, zero)))
    for s in range(2):
        table = legendre_ref[s]
        plain_ref[s] = table.astype(jnp.bfloat16)
        table = table * weight_ref[...]
        high = table.astype(jnp.bfloat16)
        weighted_ref[0, s] = high
        weighted_ref[1, s] = (table - high.astype(jnp.float32)).astype(jnp.bfloat16)

    def recur_blocks(part, first, last):
        def one(g, carry):
            left = jnp.concatenate(
                [states_ref[index_ref[g, l]] for l in range(CONN)],
                axis=1,
            )
            right = jnp.concatenate([blocks_ref[g, l] for l in range(CONN)], axis=1)
            recur_ref[:, pl.ds(pl.multiple_of(g * BLOCK, BLOCK), BLOCK)] = lax.dot_general(
                left, right, (((1,), (1,)), ((), ())), preferred_element_type=jnp.float32
            )
            return carry

        lax.fori_loop(first, last, one, 0)
        columns = pl.ds(first * BLOCK, (last - first) * BLOCK)
        copy = pltpu.make_async_copy(
            recur_ref.at[:, columns], recur_hbm.at[:, columns], store_sem.at[part]
        )
        copy.start()
        return copy

    load_states(0).wait()
    each(RES // BLOCK, lambda b: load_states(b).wait())
    load_blocks.wait()
    stores = [recur_blocks(0, 0, SPLIT[0])]
    each(LONS, lambda s: row_copy(s).wait_recv())

    data = rows_ref[...].reshape(LONS, SUB_ROWS, BAND, CHANNELS)
    data = jnp.concatenate(
        [data[:, r].reshape(COLS, CHANNELS) for r in range(SUB_ROWS)], axis=1
    )

    def transform(part):
        at = pl.ds(pl.multiple_of(part * WAVES, WAVES), WAVES)
        return jnp.dot(
            table_ref[0, at, :], data, preferred_element_type=jnp.float32
        ) + jnp.dot(table_ref[1, at, :], data, preferred_element_type=jnp.float32)

    zonal_ref[...] = transform(1 - core).astype(jnp.bfloat16)
    to_sibling = pltpu.make_async_remote_copy(
        src_ref=zonal_ref,
        dst_ref=sibling_ref,
        send_sem=core_send.at[0],
        recv_sem=core_recv.at[0],
        device_id=sibling,
        device_id_type=MESH,
    )
    to_sibling.start()
    own = transform(core)
    to_sibling.wait_recv()
    got = sibling_ref[...].astype(jnp.float32)
    lower = jnp.where(core == 0, own, got).reshape(CHIPS, 4, LANES)
    upper = jnp.where(core == 0, got, own).reshape(CHIPS, 4, LANES)
    message_ref[...] = jnp.concatenate([lower, upper], axis=1).astype(jnp.bfloat16)

    def out_copy(s):
        return pltpu.make_async_remote_copy(
            src_ref=message_ref.at[chip_at(s)],
            dst_ref=owned_ref.at[chip],
            send_sem=out_send.at[s],
            recv_sem=out_recv.at[s],
            device_id=chip_device(s),
            device_id_type=MESH,
        )

    each(CHIPS, lambda s: out_copy(s).start())
    owned_ref[chip] = message_ref[chip]

    entry = lax.broadcasted_iota(jnp.int32, (2 * WAVES, WAVES), 0)
    for half in range(2):
        chosen = jnp.where(
            entry == row_ref[:, half * WAVES : (half + 1) * WAVES], 1.0, 0.0
        ).astype(jnp.bfloat16)
        inverted_ref[half] = jnp.dot(
            inverse_ref[...], chosen, preferred_element_type=jnp.float32
        ).astype(jnp.bfloat16)
    stores.append(recur_blocks(1, SPLIT[0], SPLIT[1]))
    each(CHIPS, lambda s: out_copy(s).wait_recv())

    for r in range(SUB_ROWS):
        wide_ref[r] = (
            owned_ref[:, :, r * 128 : (r + 1) * 128]
            .astype(jnp.float32)
            .reshape(CHIPS * 8, CHANNELS)
        )
    scaled = level * (level + 1.0) / float((WAVES - 1) * WAVES)
    damping = 1.0 / (1.0 + diffusion_ref[...] * (scaled * scaled))
    damping = jnp.concatenate([damping, damping], axis=1)
    for s in range(2):
        zonal = jnp.concatenate(
            [
                jnp.concatenate(
                    [
                        wide_ref[r, pl.ds(4 * h + 2 * s + p, CHIPS, stride=8), :]
                        for r in range(SUB_ROWS)
                        for h in range(2)
                    ],
                    axis=0,
                )
                for p in range(2)
            ],
            axis=1,
        ).astype(jnp.bfloat16)
        filtered = damping * (
            jnp.dot(weighted_ref[0, s], zonal, preferred_element_type=jnp.float32)
            + jnp.dot(weighted_ref[1, s], zonal, preferred_element_type=jnp.float32)
        )
        for p in range(2):
            spectral_ref[s, p] = filtered[:, p * 128 : (p + 1) * 128]
        grid = lax.dot_general(
            plain_ref[s],
            filtered.astype(jnp.bfloat16),
            (((0,), (0,)), ((), ())),
            preferred_element_type=jnp.float32,
        )
        for p in range(2):
            for r in range(SUB_ROWS):
                for h in range(2):
                    at = r * 128 + h * CHIPS
                    back_ref[r, pl.ds(4 * h + 2 * s + p, CHIPS, stride=8), :] = grid[
                        at : at + CHIPS, p * 128 : (p + 1) * 128
                    ]
    for r in range(SUB_ROWS):
        reply_ref[:, :, r * 128 : (r + 1) * 128] = (
            back_ref[r].reshape(CHIPS, 8, CHANNELS).astype(jnp.bfloat16)
        )

    def back_copy(s):
        return pltpu.make_async_remote_copy(
            src_ref=reply_ref.at[chip_at(s)],
            dst_ref=replied_ref.at[chip],
            send_sem=back_send.at[s],
            recv_sem=back_recv.at[s],
            device_id=chip_device(s),
            device_id_type=MESH,
        )

    each(CHIPS, lambda s: back_copy(s).start())
    replied_ref[chip] = reply_ref[chip]
    stores.append(recur_blocks(2, SPLIT[1], SPLIT[2]))
    each(CHIPS, lambda s: back_copy(s).wait_recv())

    whole = replied_ref[...].astype(jnp.float32)
    lower = whole[:, 0:4].reshape(2 * CHIPS * 2, LANES)
    upper = whole[:, 4:8].reshape(2 * CHIPS * 2, LANES)
    other_ref[...] = jnp.where(core == 0, upper, lower).astype(jnp.bfloat16)
    for_sibling = pltpu.make_async_remote_copy(
        src_ref=other_ref,
        dst_ref=mine_ref,
        send_sem=core_send.at[1],
        recv_sem=core_recv.at[1],
        device_id=sibling,
        device_id_type=MESH,
    )
    for_sibling.start()
    kept = jnp.where(core == 0, lower, upper).astype(jnp.bfloat16)
    own = jnp.dot(inverted_ref[core], kept, preferred_element_type=jnp.float32)
    for_sibling.wait_recv()
    own += jnp.dot(inverted_ref[1 - core], mine_ref[...], preferred_element_type=jnp.float32)
    for d in range(LONS):
        samples_ref[d] = own[d * SENT_COLS : (d + 1) * SENT_COLS].astype(jnp.bfloat16)

    def grid_copy(s):
        return pltpu.make_async_remote_copy(
            src_ref=samples_ref.at[lon_at(s)],
            dst_ref=framed_ref.at[o],
            send_sem=grid_send.at[s],
            recv_sem=grid_recv.at[s],
            device_id=(a, lon_at(s)),
            device_id_type=MESH,
        )

    each(LONS, lambda s: grid_copy(s).start())
    framed_ref[o] = samples_ref[o]
    stores.append(recur_blocks(3, SPLIT[2], SPLIT[3]))
    each(LONS, lambda s: grid_copy(s).wait_recv())

    up = pltpu.make_async_remote_copy(
        src_ref=framed_ref.at[LONS - 1, :, pl.ds(CHANNELS, 2 * CHANNELS)],
        dst_ref=halo_ref.at[0],
        send_sem=halo_send.at[0],
        recv_sem=halo_recv.at[0],
        device_id=(lax.rem(a + 1, LATS), o),
        device_id_type=MESH,
    )
    down = pltpu.make_async_remote_copy(
        src_ref=framed_ref.at[0, :, pl.ds(0, 2 * CHANNELS)],
        dst_ref=halo_ref.at[1],
        send_sem=halo_send.at[1],
        recv_sem=halo_recv.at[1],
        device_id=(lax.rem(a + LATS - 1, LATS), o),
        device_id_type=MESH,
    )

    @pl.when(a < LATS - 1)
    def _():
        up.start()

    @pl.when(a > 0)
    def _():
        down.start()

    each(LONS, lambda s: row_copy(s).wait_send())
    each(CHIPS, lambda s: out_copy(s).wait_send())
    each(CHIPS, lambda s: back_copy(s).wait_send())
    each(LONS, lambda s: grid_copy(s).wait_send())
    to_sibling.wait_send()
    for_sibling.wait_send()
    for copy in stores:
        copy.wait()

    @pl.when(a < LATS - 1)
    def _():
        up.wait_send()
        down.wait_recv()

    @pl.when(a > 0)
    def _():
        down.wait_send()
        up.wait_recv()


def reservoir_kernel(
    rows_ref,
    halo_ref,
    recur_ref,
    node_ref,
    gain_ref,
    readout_ref,
    blend_ref,
    next_ref,
    frame_ref,
    drive_ref,
    total_ref,
):
    chunk = pl.program_id(0)

    @pl.when(chunk == 0)
    def _():
        def row_of(position):
            if position < 2:
                part = halo_ref[0, :, position * 128 : (position + 1) * 128]
            elif position >= BAND + 2:
                at = position - BAND - 2
                part = halo_ref[1, :, at * 128 : (at + 1) * 128]
            else:
                j = position - 2
                at = j % SUB_ROWS
                part = rows_ref[j // SUB_ROWS, :, at * 128 : (at + 1) * 128]
            return part.astype(jnp.float32)

        for pair in range(FRAME // 2):
            for a in range(2):
                upper = row_of(4 * pair + a)
                lower = row_of(4 * pair + 2 + a)
                for b in range(WINDOW):
                    start = (b % 2) * HALF + b // 2
                    both = jnp.concatenate(
                        [upper[start : start + TILES], lower[start : start + TILES]], axis=0
                    )
                    at = (b * 2 + a) * 128
                    frame_ref[pair * 48 : (pair + 1) * 48, at : at + 128] = both.astype(
                        jnp.bfloat16
                    )
        total_ref[...] = jnp.zeros_like(total_ref)

    entry = lax.broadcasted_iota(jnp.int32, (PICK, CHUNK), 0)
    pick = jnp.where(entry == node_ref[1:2, :], 1.0, 0.0).astype(jnp.bfloat16)
    drive_ref[...] = jnp.dot(frame_ref[...], pick, preferred_element_type=jnp.float32)
    count = TILES * TILES
    row = node_ref[0:1, :]
    picked = jnp.where(
        row == 0,
        drive_ref[0:count],
        jnp.where(row == 1, drive_ref[TILES : count + TILES], drive_ref[2 * TILES :]),
    )
    upcoming = jnp.tanh(recur_ref[...] + picked * gain_ref[0:1, :] + gain_ref[1:2, :]).astype(
        jnp.bfloat16
    )
    next_ref[...] = upcoming
    total_ref[...] += jnp.dot(upcoming, readout_ref[...], preferred_element_type=jnp.float32)

    @pl.when(chunk == CHUNKS - 1)
    def _():
        for a in range(2):
            for b in range(2):
                at = ((2 + b) * 2 + a) * 128
                forecast = frame_ref[:, at : at + 128].astype(jnp.float32)
                to = (a * 2 + b) * 128
                for i in range(TILES):
                    blend_ref[pl.ds((2 * i + a) * BAND + b, TILES, stride=2), :] = (
                        forecast[(i + 1) * TILES : (i + 2) * TILES]
                        + total_ref[i * TILES : (i + 1) * TILES, to : to + 128]
                    )


def shards(
    fields,
    diffusion,
    wave_slots,
    reservoir_state,
    adjacency_blocks,
    adjacency_index,
    input_index,
    input_gain,
    bias,
    readout,
):
    vmem = pl.BlockSpec(memory_space=pltpu.VMEM)
    smem = pl.BlockSpec(memory_space=pltpu.SMEM)
    hbm = pl.BlockSpec(memory_space=pl.ANY)
    bf16 = functools.partial(pltpu.VMEM, dtype=jnp.bfloat16)
    f32 = functools.partial(pltpu.VMEM, dtype=jnp.float32)

    order = wave_slots.reshape(CHIPS, 2, 2).transpose(1, 0, 2).reshape(-1, 1)
    slot_part = (2 * order + jnp.arange(2, dtype=jnp.int32)).reshape(-1)
    forward_high, forward_low = split(forward_rows().astype(np.float32))
    cos_col, sin_col = geometry()
    spectral, framed, halo, recur = pl.pallas_call(
        chain_kernel,
        out_shape=(
            jax.ShapeDtypeStruct((2, 2, WAVES, CHANNELS), jnp.float32),
            jax.ShapeDtypeStruct((LONS, SENT_COLS, LANES), jnp.bfloat16),
            jax.ShapeDtypeStruct((2, SENT_COLS, 2 * CHANNELS), jnp.bfloat16),
            jax.ShapeDtypeStruct((NODES, RES), jnp.float32),
        ),
        in_specs=[smem] * 2 + [vmem] * 11 + [hbm] * 2,
        out_specs=(vmem, vmem, vmem, hbm),
        scratch_shapes=[
            bf16((RES // BLOCK, NODES, BLOCK)),
            bf16((RES // BLOCK, CONN, BLOCK, BLOCK)),
            f32((NODES, RES)),
            bf16((LONS, SUB_ROWS * BAND, CHANNELS)),
            bf16((LONS, SUB_ROWS * BAND, CHANNELS)),
            bf16((2, 2 * WAVES, COLS)),
            f32((2, 3, WAVES, CHANNELS)),
            f32((2, WAVES, ROWS)),
            bf16((2, 2, WAVES, ROWS)),
            bf16((2, WAVES, ROWS)),
            bf16((WAVES, LANES)),
            bf16((WAVES, LANES)),
            bf16((CHIPS, 8, LANES)),
            bf16((CHIPS, 8, LANES)),
            f32((SUB_ROWS, 8 * CHIPS, CHANNELS)),
            f32((SUB_ROWS, 8 * CHIPS, CHANNELS)),
            bf16((CHIPS, 8, LANES)),
            bf16((CHIPS, 8, LANES)),
            bf16((WAVES, LANES)),
            bf16((WAVES, LANES)),
            bf16((2, LONS * SENT_COLS, WAVES)),
            bf16((LONS, SENT_COLS, LANES)),
            pltpu.SemaphoreType.DMA((RES // BLOCK + 1,)),
            pltpu.SemaphoreType.DMA((4,)),
            pltpu.SemaphoreType.DMA((LONS,)),
            pltpu.SemaphoreType.DMA((LONS,)),
            pltpu.SemaphoreType.DMA((2,)),
            pltpu.SemaphoreType.DMA((2,)),
            pltpu.SemaphoreType.DMA((CHIPS,)),
            pltpu.SemaphoreType.DMA((CHIPS,)),
            pltpu.SemaphoreType.DMA((CHIPS,)),
            pltpu.SemaphoreType.DMA((CHIPS,)),
            pltpu.SemaphoreType.DMA((LONS,)),
            pltpu.SemaphoreType.DMA((LONS,)),
            pltpu.SemaphoreType.DMA((2,)),
            pltpu.SemaphoreType.DMA((2,)),
        ],
        compiler_params=pltpu.CompilerParams(
            collective_id=0, has_side_effects=True, vmem_limit_bytes=56 * MB
        ),
        cost_estimate=pl.CostEstimate(
            flops=2 * NODES * RES * CONN * BLOCK, bytes_accessed=30 * MB, transcendentals=0
        ),
        name="chain",
    )(
        wave_slots,
        adjacency_index,
        fields.reshape(BAND * BAND, CHANNELS),
        slot_part[:, None],
        slot_part[None, :],
        jnp.asarray(forward_high),
        jnp.asarray(forward_low),
        jnp.asarray(inverse_columns(), jnp.bfloat16),
        jnp.asarray(cos_col[None, :], jnp.float32),
        jnp.asarray(np.log(sin_col)[None, :], jnp.float32),
        jnp.asarray((math.pi / ROWS) * sin_col[None, :], jnp.float32),
        diffusion[None, :],
        jnp.asarray(log_terms()[None, :], jnp.float32),
        reservoir_state.reshape(NODES, RES),
        adjacency_blocks,
    )

    row_at = input_index // (WINDOW * CHANNELS)
    col_at = input_index // CHANNELS % WINDOW
    key = (col_at * 2 + row_at % 2) * CHANNELS + input_index % CHANNELS
    const = lambda *zeros: (lambda c: zeros)
    blended, upcoming = pl.pallas_call(
        reservoir_kernel,
        grid=(CHUNKS,),
        out_shape=(
            jax.ShapeDtypeStruct((BAND * BAND, CHANNELS), jnp.float32),
            jax.ShapeDtypeStruct((NODES, RES), jnp.bfloat16),
        ),
        in_specs=[
            pl.BlockSpec((LONS, SENT_COLS, LANES), const(0, 0, 0)),
            pl.BlockSpec((2, SENT_COLS, 2 * CHANNELS), const(0, 0, 0)),
            pl.BlockSpec((NODES, CHUNK), lambda c: (0, c)),
            pl.BlockSpec((2, CHUNK), lambda c: (0, c)),
            pl.BlockSpec((2, CHUNK), lambda c: (0, c)),
            pl.BlockSpec((CHUNK, 4 * CHANNELS), lambda c: (c, 0)),
        ],
        out_specs=(
            pl.BlockSpec((BAND * BAND, CHANNELS), const(0, 0)),
            pl.BlockSpec((NODES, CHUNK), lambda c: (0, c)),
        ),
        scratch_shapes=[
            pltpu.VMEM((FRAME * TILES, PICK), jnp.bfloat16),
            pltpu.VMEM((FRAME * TILES, CHUNK), jnp.float32),
            pltpu.VMEM((NODES, 4 * CHANNELS), jnp.float32),
        ],
        compiler_params=pltpu.CompilerParams(vmem_limit_bytes=56 * MB),
        cost_estimate=pl.CostEstimate(
            flops=2 * FRAME * TILES * RES * PICK,
            bytes_accessed=24 * MB,
            transcendentals=NODES * RES,
        ),
        name="reservoir",
    )(
        framed,
        halo,
        recur,
        jnp.stack([row_at // 2, key]),
        jnp.stack([input_gain, bias]),
        readout,
    )
    return (
        blended.reshape(BAND, BAND, CHANNELS),
        upcoming.reshape(TILES, TILES, RES),
        spectral,
    )


def solution(mesh):
    placed = (P("lat", "lon", None), P(), P(), P("lat", "lon", None), P(), P(), P(), P(), P(), P())
    return jax.shard_map(
        shards,
        mesh=mesh,
        in_specs=placed,
        out_specs=(
            P("lat", "lon", None),
            P("lat", "lon", None),
            P(("lat", "lon"), None, None, None),
        ),
        check_vma=False,
    )
```

```python
import functools
import math

import jax
import jax.numpy as jnp
import numpy as np
from jax import lax
from jax.experimental import pallas as pl
from jax.experimental.pallas import tpu as pltpu
from jax.sharding import PartitionSpec as P

ROWS = 384
COLS = 768
WAVES = 256
CHANNELS = 128
RES = 4096
BLOCK = 128
CONN = 8
TILE = 2
WINDOW = 6
LATS = 8
LONS = 16
DEVICES = LATS * LONS
CHIPS = DEVICES // 2
SUB_ROWS = ROWS // DEVICES
BAND = 48
HALF = 28
SENT_COLS = 2 * HALF
TILES = 24
FRAME = TILES + 2
CHUNK = 512
CHUNKS = RES // CHUNK
FRAME_ROWS = 736
MB = 1 << 20
MESH = pl.DeviceIdType.MESH
SPLIT = (7, 16, 24, 32)
LANES = SUB_ROWS * CHANNELS
NODES = TILES * TILES


def geometry():
    j = np.arange(ROWS).reshape(CHIPS, 2, SUB_ROWS).transpose(2, 1, 0).reshape(-1)
    colatitude = (j + 0.5) * (math.pi / ROWS)
    return np.cos(colatitude), np.sin(colatitude)


def log_terms():
    index = np.arange(WAVES).astype(np.float64)
    return np.where(index > 0, np.log1p(0.5 / np.maximum(index, 1.0)), 0.0)


def forward_rows():
    m = np.arange(WAVES)[:, None]
    k = np.arange(COLS)[None, :]
    angle = (m * k % COLS) * (2.0 * math.pi / COLS)
    table = np.stack([np.cos(angle), -np.sin(angle)], axis=1) / COLS
    return table.reshape(2 * WAVES, COLS)


def inverse_columns():
    o = np.arange(LONS)[:, None, None]
    b = np.arange(2)[None, :, None]
    t = np.arange(HALF)[None, None, :]
    k = ((BAND * o - 2 + 2 * t + b) % COLS).reshape(-1)
    m = np.arange(WAVES)[None, :]
    angle = (m * k[:, None] % COLS) * (2.0 * math.pi / COLS)
    factor = np.where(m == 0, 1.0, 2.0)
    table = np.stack([factor * np.cos(angle), -factor * np.sin(angle)], axis=2)
    return table.reshape(LONS * SENT_COLS, 2 * WAVES)


def split(table):
    high = table.astype(jnp.bfloat16)
    return high, (table - high.astype(np.float32)).astype(jnp.bfloat16)


def chain_kernel(
    slots_ref,
    index_ref,
    fields_ref,
    order_ref,
    forward_high_ref,
    forward_low_ref,
    inverse_ref,
    cos_ref,
    log_sin_ref,
    weight_ref,
    diffusion_ref,
    logs_ref,
    states_hbm,
    blocks_hbm,
    spectral_ref,
    framed_ref,
    halo_ref,
    recur_hbm,
    states_ref,
    blocks_ref,
    recur_ref,
    sent_ref,
    rows_ref,
    chosen_ref,
    table_ref,
    factor_ref,
    legendre_ref,
    weighted_ref,
    plain_ref,
    zonal_ref,
    sibling_ref,
    message_ref,
    owned_ref,
    wide_ref,
    back_ref,
    reply_ref,
    replied_ref,
    mine_ref,
    other_ref,
    inverted_ref,
    samples_ref,
    load_sem,
    store_sem,
    lon_send,
    lon_recv,
    core_send,
    core_recv,
    out_send,
    out_recv,
    back_send,
    back_recv,
    grid_send,
    grid_recv,
    halo_send,
    halo_recv,
):
    a = lax.axis_index("lat")
    o = lax.axis_index("lon")
    core = lax.rem(o, 2)
    chip = a * (LONS // 2) + lax.div(o, 2)
    sibling = (a, o + 1 - 2 * core)

    def along(digit):
        half = lax.div(digit, 2)
        return (1 - half) * (2 - digit) + half * 3 * (3 - digit)

    def moved(at, size, by):
        return lax.rem(at + by, size)

    def lon_at(step):
        z = moved(lax.div(o, 8), 2, 1 - lax.div(step, 8))
        y = moved(lax.rem(lax.div(o, 2), 4), 4, along(lax.rem(lax.div(step, 2), 4)))
        return z * 8 + y * 2 + moved(core, 2, 1 - lax.rem(step, 2))

    def chip_at(step):
        z_hi = moved(lax.div(o, 8), 2, 1 - lax.div(step, 32))
        x = moved(lax.rem(a, 4), 4, along(lax.rem(lax.div(step, 8), 4)))
        y = moved(lax.rem(lax.div(o, 2), 4), 4, along(lax.rem(lax.div(step, 2), 4)))
        z_lo = moved(lax.div(a, 4), 2, 1 - lax.rem(step, 2))
        return (z_lo * 4 + x) * 8 + z_hi * 4 + y

    def chip_device(step):
        other = chip_at(step)
        return (lax.div(other, LONS // 2), 2 * lax.rem(other, LONS // 2) + core)

    def each(count, action):
        def step(s, carry):
            action(s)
            return carry

        lax.fori_loop(0, count - 1, step, 0)

    def load_states(b):
        return pltpu.make_async_copy(
            states_hbm.at[:, pl.ds(pl.multiple_of(b * BLOCK, BLOCK), BLOCK)],
            states_ref.at[b],
            load_sem.at[b],
        )

    load_blocks = pltpu.make_async_copy(blocks_hbm, blocks_ref, load_sem.at[RES // BLOCK])

    barrier = pltpu.get_barrier_semaphore()
    each(
        CHIPS,
        lambda s: pl.semaphore_signal(
            barrier, inc=1, device_id=chip_device(s), device_id_type=MESH
        ),
    )
    each(
        LONS,
        lambda s: pl.semaphore_signal(
            barrier, inc=1, device_id=(a, lon_at(s)), device_id_type=MESH
        ),
    )
    load_blocks.start()
    each(RES // BLOCK + 1, lambda b: load_states(b).start())
    halo_ref[...] = jnp.zeros_like(halo_ref)
    for d in range(LONS):
        sent_ref[d] = fields_ref[d * 144 : (d + 1) * 144, :].astype(jnp.bfloat16)
    pl.semaphore_wait(barrier, LONS + CHIPS - 2)

    def row_copy(s):
        return pltpu.make_async_remote_copy(
            src_ref=sent_ref.at[lon_at(s)],
            dst_ref=rows_ref.at[o],
            send_sem=lon_send.at[s],
            recv_sem=lon_recv.at[s],
            device_id=(a, lon_at(s)),
            device_id_type=MESH,
        )

    each(LONS, lambda s: row_copy(s).start())
    rows_ref[o] = sent_ref[o]

    column = lax.broadcasted_iota(jnp.int32, (WAVES, 2 * WAVES), 1)
    slot = 4 * ((column >> 2) & (CHIPS - 1)) + 2 * (column >> 8) + ((column >> 1) & 1)
    moves = jnp.where(lax.broadcasted_iota(jnp.int32, slot.shape, 0) == slot, 1.0, 0.0)
    waves = jnp.broadcast_to(order_ref[...].astype(jnp.float32), (8, WAVES))
    waves = jnp.dot(
        waves.astype(jnp.bfloat16),
        moves.astype(jnp.bfloat16),
        preferred_element_type=jnp.float32,
    ).astype(jnp.int32)
    key = 2 * waves[0:1] + (column[0:1] & 1)
    entry = lax.broadcasted_iota(jnp.int32, (2 * WAVES, 2 * WAVES), 0)
    chosen_ref[...] = jnp.where(entry == key, 1.0, 0.0).astype(jnp.bfloat16)
    for half, source in enumerate((forward_high_ref, forward_low_ref)):
        table_ref[half] = lax.dot_general(
            chosen_ref[...],
            source[...],
            (((0,), (0,)), ((), ())),
            preferred_element_type=jnp.float32,
        ).astype(jnp.bfloat16)

    level = lax.broadcasted_iota(jnp.int32, (WAVES, CHANNELS), 0).astype(jnp.float32)
    cos_col = cos_ref[...]
    poles = []
    for s in range(2):
        m = slots_ref[2 * (a * LONS + o) + s]
        order = m.astype(jnp.float32)
        above = level > order
        order_sq = order * order
        prior = level - 1.0
        factor = jnp.sqrt(
            jnp.where(above, 4.0 * level * level - 1.0, 0.0)
            / jnp.where(above, level * level - order_sq, 1.0)
        )
        factor_ref[s, 0] = factor
        factor_ref[s, 1] = factor * jnp.sqrt(
            jnp.where(above, prior * prior - order_sq, 0.0)
            / jnp.where(level > 1.5, 4.0 * prior * prior - 1.0, 1.0)
        )
        factor_ref[s, 2] = jnp.where(level == order, 1.0, 0.0)
        index = lax.broadcasted_iota(jnp.int32, (1, WAVES), 1)
        logs = jnp.sum(jnp.where(index <= m, logs_ref[...], 0.0), axis=1, keepdims=True)
        poles.append(
            jnp.exp(0.5 * logs + order * log_sin_ref[...] - 0.5 * math.log(2.0))
        )

    def eight(base, carry):
        state = list(carry)
        at = pl.ds(pl.multiple_of(base * 8, 8), 8)
        for s in range(2):
            previous, current = state[s]
            factors = [factor_ref[s, f, at, :] for f in range(3)]
            stacked = []
            for step in range(8):
                row, drop, first = [
                    jnp.concatenate([f[step : step + 1]] * SUB_ROWS, axis=1) for f in factors
                ]
                value = row * (cos_col * current) - drop * previous + first * poles[s]
                previous, current = current, value
                stacked.append(value)
            state[s] = (previous, current)
            legendre_ref[s, at, :] = jnp.concatenate(stacked, axis=0)
        return tuple(state)

    zero = jnp.zeros((1, ROWS), jnp.float32)
    lax.fori_loop(0, WAVES // 8, eight, ((zero, zero), (zero, zero)))
    for s in range(2):
        table = legendre_ref[s]
        plain_ref[s] = table.astype(jnp.bfloat16)
        table = table * weight_ref[...]
        high = table.astype(jnp.bfloat16)
        weighted_ref[0, s] = high
        weighted_ref[1, s] = (table - high.astype(jnp.float32)).astype(jnp.bfloat16)

    def recur_blocks(part, first, last):
        def one(g, carry):
            left = jnp.concatenate(
                [states_ref[index_ref[l, g]] for l in range(CONN)],
                axis=1,
            )
            right = jnp.concatenate([blocks_ref[g, l] for l in range(CONN)], axis=1)
            recur_ref[:, pl.ds(pl.multiple_of(g * BLOCK, BLOCK), BLOCK)] = lax.dot_general(
                left, right, (((1,), (1,)), ((), ())), preferred_element_type=jnp.float32
            )
            return carry

        lax.fori_loop(first, last, one, 0)
        columns = pl.ds(first * BLOCK, (last - first) * BLOCK)
        copy = pltpu.make_async_copy(
            recur_ref.at[:, columns], recur_hbm.at[:, columns], store_sem.at[part]
        )
        copy.start()
        return copy

    each(RES // BLOCK + 1, lambda b: load_states(b).wait())
    load_blocks.wait()
    stores = [recur_blocks(0, 0, SPLIT[0])]
    each(LONS, lambda s: row_copy(s).wait_recv())

    data = rows_ref[...].reshape(LONS, SUB_ROWS, BAND, CHANNELS)
    data = jnp.concatenate(
        [data[:, r].reshape(COLS, CHANNELS) for r in range(SUB_ROWS)], axis=1
    )

    def transform(part):
        at = pl.ds(pl.multiple_of(part * WAVES, WAVES), WAVES)
        return jnp.dot(
            table_ref[0, at, :], data, preferred_element_type=jnp.float32
        ) + jnp.dot(table_ref[1, at, :], data, preferred_element_type=jnp.float32)

    zonal_ref[...] = transform(1 - core).astype(jnp.bfloat16)
    to_sibling = pltpu.make_async_remote_copy(
        src_ref=zonal_ref,
        dst_ref=sibling_ref,
        send_sem=core_send.at[0],
        recv_sem=core_recv.at[0],
        device_id=sibling,
        device_id_type=MESH,
    )
    to_sibling.start()
    own = transform(core)
    to_sibling.wait_recv()
    got = sibling_ref[...].astype(jnp.float32)
    lower = jnp.where(core == 0, own, got).reshape(CHIPS, 4, LANES)
    upper = jnp.where(core == 0, got, own).reshape(CHIPS, 4, LANES)
    message_ref[...] = jnp.concatenate([lower, upper], axis=1).astype(jnp.bfloat16)

    def out_copy(s):
        return pltpu.make_async_remote_copy(
            src_ref=message_ref.at[chip_at(s)],
            dst_ref=owned_ref.at[chip],
            send_sem=out_send.at[s],
            recv_sem=out_recv.at[s],
            device_id=chip_device(s),
            device_id_type=MESH,
        )

    each(CHIPS, lambda s: out_copy(s).start())
    owned_ref[chip] = message_ref[chip]

    for half in range(2):
        inverted_ref[half] = jnp.dot(
            inverse_ref[...],
            chosen_ref[:, half * WAVES : (half + 1) * WAVES],
            preferred_element_type=jnp.float32,
        ).astype(jnp.bfloat16)
    stores.append(recur_blocks(1, SPLIT[0], SPLIT[1]))
    each(CHIPS, lambda s: out_copy(s).wait_recv())

    for r in range(SUB_ROWS):
        wide_ref[r] = (
            owned_ref[:, :, r * 128 : (r + 1) * 128]
            .astype(jnp.float32)
            .reshape(CHIPS * 8, CHANNELS)
        )
    scaled = level * (level + 1.0) / float((WAVES - 1) * WAVES)
    damping = 1.0 / (1.0 + diffusion_ref[...] * (scaled * scaled))
    damping = jnp.concatenate([damping, damping], axis=1)
    for s in range(2):
        zonal = jnp.concatenate(
            [
                jnp.concatenate(
                    [
                        wide_ref[r, pl.ds(4 * h + 2 * s + p, CHIPS, stride=8), :]
                        for r in range(SUB_ROWS)
                        for h in range(2)
                    ],
                    axis=0,
                )
                for p in range(2)
            ],
            axis=1,
        ).astype(jnp.bfloat16)
        filtered = damping * (
            jnp.dot(weighted_ref[0, s], zonal, preferred_element_type=jnp.float32)
            + jnp.dot(weighted_ref[1, s], zonal, preferred_element_type=jnp.float32)
        )
        for p in range(2):
            spectral_ref[s, p] = filtered[:, p * 128 : (p + 1) * 128]
        grid = lax.dot_general(
            plain_ref[s],
            filtered.astype(jnp.bfloat16),
            (((0,), (0,)), ((), ())),
            preferred_element_type=jnp.float32,
        )
        for p in range(2):
            for r in range(SUB_ROWS):
                for h in range(2):
                    at = r * 128 + h * CHIPS
                    back_ref[r, pl.ds(4 * h + 2 * s + p, CHIPS, stride=8), :] = grid[
                        at : at + CHIPS, p * 128 : (p + 1) * 128
                    ]
    for r in range(SUB_ROWS):
        reply_ref[:, :, r * 128 : (r + 1) * 128] = (
            back_ref[r].reshape(CHIPS, 8, CHANNELS).astype(jnp.bfloat16)
        )

    def back_copy(s):
        return pltpu.make_async_remote_copy(
            src_ref=reply_ref.at[chip_at(s)],
            dst_ref=replied_ref.at[chip],
            send_sem=back_send.at[s],
            recv_sem=back_recv.at[s],
            device_id=chip_device(s),
            device_id_type=MESH,
        )

    each(CHIPS, lambda s: back_copy(s).start())
    replied_ref[chip] = reply_ref[chip]
    stores.append(recur_blocks(2, SPLIT[1], SPLIT[2]))
    each(CHIPS, lambda s: back_copy(s).wait_recv())

    whole = replied_ref[...].astype(jnp.float32)
    lower = whole[:, 0:4].reshape(2 * CHIPS * 2, LANES)
    upper = whole[:, 4:8].reshape(2 * CHIPS * 2, LANES)
    other_ref[...] = jnp.where(core == 0, upper, lower).astype(jnp.bfloat16)
    for_sibling = pltpu.make_async_remote_copy(
        src_ref=other_ref,
        dst_ref=mine_ref,
        send_sem=core_send.at[1],
        recv_sem=core_recv.at[1],
        device_id=sibling,
        device_id_type=MESH,
    )
    for_sibling.start()
    kept = jnp.where(core == 0, lower, upper).astype(jnp.bfloat16)
    own = jnp.dot(inverted_ref[core], kept, preferred_element_type=jnp.float32)
    for_sibling.wait_recv()
    own += jnp.dot(inverted_ref[1 - core], mine_ref[...], preferred_element_type=jnp.float32)
    for d in range(LONS):
        samples_ref[d] = own[d * SENT_COLS : (d + 1) * SENT_COLS].astype(jnp.bfloat16)

    def grid_copy(s):
        return pltpu.make_async_remote_copy(
            src_ref=samples_ref.at[lon_at(s)],
            dst_ref=framed_ref.at[o],
            send_sem=grid_send.at[s],
            recv_sem=grid_recv.at[o],
            device_id=(a, lon_at(s)),
            device_id_type=MESH,
        )

    def grid_from(source):
        return pltpu.make_async_remote_copy(
            src_ref=samples_ref.at[source],
            dst_ref=framed_ref.at[source],
            send_sem=grid_send.at[LONS - 1],
            recv_sem=grid_recv.at[source],
            device_id=(a, source),
            device_id_type=MESH,
        )

    each(LONS, lambda s: grid_copy(s).start())
    framed_ref[o] = samples_ref[o]
    stores.append(recur_blocks(3, SPLIT[2], SPLIT[3]))
    up = pltpu.make_async_remote_copy(
        src_ref=framed_ref.at[LONS - 1, :, pl.ds(CHANNELS, 2 * CHANNELS)],
        dst_ref=halo_ref.at[0],
        send_sem=halo_send.at[0],
        recv_sem=halo_recv.at[0],
        device_id=(lax.rem(a + 1, LATS), o),
        device_id_type=MESH,
    )
    down = pltpu.make_async_remote_copy(
        src_ref=framed_ref.at[0, :, pl.ds(0, 2 * CHANNELS)],
        dst_ref=halo_ref.at[1],
        send_sem=halo_send.at[1],
        recv_sem=halo_recv.at[1],
        device_id=(lax.rem(a + LATS - 1, LATS), o),
        device_id_type=MESH,
    )

    @pl.when(o < LONS - 1)
    def _():
        grid_from(LONS - 1).wait_recv()

    @pl.when(a < LATS - 1)
    def _():
        up.start()

    @pl.when(o > 0)
    def _():
        grid_from(0).wait_recv()

    @pl.when(a > 0)
    def _():
        down.start()

    def arrived(source, carry):
        @pl.when(source != o)
        def _():
            grid_from(source).wait_recv()

        return carry

    lax.fori_loop(1, LONS - 1, arrived, 0)
    each(LONS, lambda s: row_copy(s).wait_send())
    each(CHIPS, lambda s: out_copy(s).wait_send())
    each(CHIPS, lambda s: back_copy(s).wait_send())
    each(LONS, lambda s: grid_copy(s).wait_send())
    to_sibling.wait_send()
    for_sibling.wait_send()
    for copy in stores:
        copy.wait()

    @pl.when(a < LATS - 1)
    def _():
        up.wait_send()
        down.wait_recv()

    @pl.when(a > 0)
    def _():
        down.wait_send()
        up.wait_recv()


def reservoir_kernel(
    rows_ref,
    halo_ref,
    recur_ref,
    entry_ref,
    gain_ref,
    bias_ref,
    readout_ref,
    coefficients_ref,
    blend_ref,
    next_ref,
    spectral_ref,
    frame_ref,
    drive_ref,
    total_ref,
):
    chunk = pl.program_id(0)
    spectral_ref[...] = coefficients_ref[...]

    @pl.when(chunk == 0)
    def _():
        def row_of(position):
            if position < 2:
                part = halo_ref[0, :, position * 128 : (position + 1) * 128]
            elif position >= BAND + 2:
                at = position - BAND - 2
                part = halo_ref[1, :, at * 128 : (at + 1) * 128]
            else:
                j = position - 2
                at = j % SUB_ROWS
                part = rows_ref[j // SUB_ROWS, :, at * 128 : (at + 1) * 128]
            return part.astype(jnp.float32)

        for group in range(0, FRAME, 4):
            for a in range(2):
                parts = [row_of(2 * i + a) for i in range(group, min(group + 4, FRAME))]
                for b in range(2):
                    block = [part[b * HALF : (b + 1) * HALF] for part in parts]
                    if len(block) < 4:
                        block.append(jnp.zeros((FRAME_ROWS - FRAME * HALF, CHANNELS), jnp.float32))
                    block = jnp.concatenate(block, axis=0)
                    at = (a * 2 + b) * 128
                    frame_ref[group * HALF : group * HALF + block.shape[0], at : at + 128] = (
                        block.astype(jnp.bfloat16)
                    )
        total_ref[...] = jnp.zeros_like(total_ref)

    index = entry_ref[...]
    place = index >> 7
    row_at = (place * 43) >> 8
    col_at = place - WINDOW * row_at
    key = ((row_at & 1) * 2 + (col_at & 1)) * CHANNELS + (index & (CHANNELS - 1))
    pick = jnp.where(
        lax.broadcasted_iota(jnp.int32, (4 * CHANNELS, CHUNK), 0) == key, 1.0, 0.0
    ).astype(jnp.bfloat16)
    drive = jnp.dot(frame_ref[...], pick, preferred_element_type=jnp.float32)
    for q in range(CHUNK // 128):
        drive_ref[q] = drive[:, q * 128 : (q + 1) * 128]
    for q in range(CHUNK // 128):
        lanes = slice(q * 128, (q + 1) * 128)
        col = jnp.broadcast_to(col_at[:, lanes] >> 1, (TILES, 128))
        row = jnp.broadcast_to(row_at[:, lanes] >> 1, (TILES, 128))
        col_one, col_two = col == 1, col == 2
        row_one, row_two = row == 1, row == 2
        gain = gain_ref[:, lanes]
        bias = bias_ref[:, lanes]

        def shifted(i):
            near, next_one, far = [
                drive_ref[q, i * HALF + k : i * HALF + k + TILES, :] for k in range(3)
            ]
            return jnp.where(col_two, far, jnp.where(col_one, next_one, near))

        kept = [shifted(0), shifted(1)]
        for i in range(0, TILES, 2):
            both = []
            for step in range(2):
                kept.append(shifted(i + step + 2))
                near, next_one, far = kept
                picked = jnp.where(row_two, far, jnp.where(row_one, next_one, near))
                kept = kept[1:]
                at = (i + step) * TILES
                both.append(jnp.tanh(recur_ref[at : at + TILES, lanes] + picked * gain + bias))
            next_ref[i * TILES : (i + 2) * TILES, lanes] = jnp.concatenate(both, axis=0).astype(
                jnp.bfloat16
            )
    total_ref[...] += jnp.dot(next_ref[...], readout_ref[...], preferred_element_type=jnp.float32)

    @pl.when(chunk == CHUNKS - 1)
    def _():
        for a in range(2):
            for b in range(2):
                at = (a * 2 + b) * 128
                forecast = frame_ref[:, at : at + 128].astype(jnp.float32)
                for i in range(TILES):
                    start = (i + 1) * HALF + 1
                    blend_ref[pl.ds((2 * i + a) * BAND + b, TILES, stride=2), :] = (
                        forecast[start : start + TILES]
                        + total_ref[i * TILES : (i + 1) * TILES, at : at + 128]
                    )


def shards(
    fields,
    diffusion,
    wave_slots,
    reservoir_state,
    adjacency_blocks,
    adjacency_index,
    input_index,
    input_gain,
    bias,
    readout,
):
    vmem = pl.BlockSpec(memory_space=pltpu.VMEM)
    smem = pl.BlockSpec(memory_space=pltpu.SMEM)
    hbm = pl.BlockSpec(memory_space=pl.ANY)
    bf16 = functools.partial(pltpu.VMEM, dtype=jnp.bfloat16)
    f32 = functools.partial(pltpu.VMEM, dtype=jnp.float32)

    forward_high, forward_low = split(forward_rows().astype(np.float32))
    cos_col, sin_col = geometry()
    spectral, framed, halo, recur = pl.pallas_call(
        chain_kernel,
        out_shape=(
            jax.ShapeDtypeStruct((2, 2, WAVES, CHANNELS), jnp.float32),
            jax.ShapeDtypeStruct((LONS, SENT_COLS, LANES), jnp.bfloat16),
            jax.ShapeDtypeStruct((2, SENT_COLS, 2 * CHANNELS), jnp.bfloat16),
            jax.ShapeDtypeStruct((NODES, RES), jnp.float32),
        ),
        in_specs=[smem] * 2 + [vmem] * 10 + [hbm] * 2,
        out_specs=(vmem, vmem, vmem, hbm),
        scratch_shapes=[
            bf16((RES // BLOCK, NODES, BLOCK)),
            bf16((RES // BLOCK, CONN, BLOCK, BLOCK)),
            f32((NODES, RES)),
            bf16((LONS, SUB_ROWS * BAND, CHANNELS)),
            bf16((LONS, SUB_ROWS * BAND, CHANNELS)),
            bf16((2 * WAVES, 2 * WAVES)),
            bf16((2, 2 * WAVES, COLS)),
            f32((2, 3, WAVES, CHANNELS)),
            f32((2, WAVES, ROWS)),
            bf16((2, 2, WAVES, ROWS)),
            bf16((2, WAVES, ROWS)),
            bf16((WAVES, LANES)),
            bf16((WAVES, LANES)),
            bf16((CHIPS, 8, LANES)),
            bf16((CHIPS, 8, LANES)),
            f32((SUB_ROWS, 8 * CHIPS, CHANNELS)),
            f32((SUB_ROWS, 8 * CHIPS, CHANNELS)),
            bf16((CHIPS, 8, LANES)),
            bf16((CHIPS, 8, LANES)),
            bf16((WAVES, LANES)),
            bf16((WAVES, LANES)),
            bf16((2, LONS * SENT_COLS, WAVES)),
            bf16((LONS, SENT_COLS, LANES)),
            pltpu.SemaphoreType.DMA((RES // BLOCK + 1,)),
            pltpu.SemaphoreType.DMA((4,)),
            pltpu.SemaphoreType.DMA((LONS,)),
            pltpu.SemaphoreType.DMA((LONS,)),
            pltpu.SemaphoreType.DMA((2,)),
            pltpu.SemaphoreType.DMA((2,)),
            pltpu.SemaphoreType.DMA((CHIPS,)),
            pltpu.SemaphoreType.DMA((CHIPS,)),
            pltpu.SemaphoreType.DMA((CHIPS,)),
            pltpu.SemaphoreType.DMA((CHIPS,)),
            pltpu.SemaphoreType.DMA((LONS,)),
            pltpu.SemaphoreType.DMA((LONS,)),
            pltpu.SemaphoreType.DMA((2,)),
            pltpu.SemaphoreType.DMA((2,)),
        ],
        compiler_params=pltpu.CompilerParams(
            collective_id=0, has_side_effects=True, vmem_limit_bytes=56 * MB
        ),
        cost_estimate=pl.CostEstimate(
            flops=2 * NODES * RES * CONN * BLOCK, bytes_accessed=30 * MB, transcendentals=0
        ),
        name="chain",
    )(
        wave_slots,
        adjacency_index.T,
        fields.reshape(BAND * BAND, CHANNELS),
        wave_slots[None, :],
        jnp.asarray(forward_high),
        jnp.asarray(forward_low),
        jnp.asarray(inverse_columns(), jnp.bfloat16),
        jnp.asarray(cos_col[None, :], jnp.float32),
        jnp.asarray(np.log(sin_col)[None, :], jnp.float32),
        jnp.asarray((math.pi / ROWS) * sin_col[None, :], jnp.float32),
        diffusion[None, :],
        jnp.asarray(log_terms()[None, :], jnp.float32),
        reservoir_state.reshape(NODES, RES),
        adjacency_blocks,
    )

    const = lambda *zeros: (lambda c: zeros)
    blended, upcoming, spectral = pl.pallas_call(
        reservoir_kernel,
        grid=(CHUNKS,),
        out_shape=(
            jax.ShapeDtypeStruct((BAND * BAND, CHANNELS), jnp.float32),
            jax.ShapeDtypeStruct((NODES, RES), jnp.bfloat16),
            jax.ShapeDtypeStruct((4 * WAVES, CHANNELS), jnp.float32),
        ),
        in_specs=[
            pl.BlockSpec((LONS, SENT_COLS, LANES), const(0, 0, 0)),
            pl.BlockSpec((2, SENT_COLS, 2 * CHANNELS), const(0, 0, 0)),
            pl.BlockSpec((NODES, CHUNK), lambda c: (0, c)),
            pl.BlockSpec((1, CHUNK), lambda c: (0, c)),
            pl.BlockSpec((1, CHUNK), lambda c: (0, c)),
            pl.BlockSpec((1, CHUNK), lambda c: (0, c)),
            pl.BlockSpec((CHUNK, 4 * CHANNELS), lambda c: (c, 0)),
            pl.BlockSpec((4 * WAVES // CHUNKS, CHANNELS), lambda c: (c, 0)),
        ],
        out_specs=(
            pl.BlockSpec((BAND * BAND, CHANNELS), const(0, 0)),
            pl.BlockSpec((NODES, CHUNK), lambda c: (0, c)),
            pl.BlockSpec((4 * WAVES // CHUNKS, CHANNELS), lambda c: (c, 0)),
        ),
        scratch_shapes=[
            pltpu.VMEM((FRAME_ROWS, 4 * CHANNELS), jnp.bfloat16),
            pltpu.VMEM((CHUNK // 128, FRAME_ROWS, 128), jnp.float32),
            pltpu.VMEM((NODES, 4 * CHANNELS), jnp.float32),
        ],
        compiler_params=pltpu.CompilerParams(vmem_limit_bytes=56 * MB),
        cost_estimate=pl.CostEstimate(
            flops=2 * (FRAME_ROWS + NODES) * RES * 4 * CHANNELS,
            bytes_accessed=24 * MB,
            transcendentals=NODES * RES,
        ),
        name="reservoir",
    )(
        framed,
        halo,
        recur,
        input_index[None, :],
        input_gain[None, :],
        bias[None, :],
        readout,
        spectral.reshape(4 * WAVES, CHANNELS),
    )
    return (
        blended.reshape(BAND, BAND, CHANNELS),
        upcoming.reshape(TILES, TILES, RES),
        spectral.reshape(2, 2, WAVES, CHANNELS),
    )


def solution(mesh):
    placed = (P("lat", "lon", None), P(), P(), P("lat", "lon", None), P(), P(), P(), P(), P(), P())
    return jax.shard_map(
        shards,
        mesh=mesh,
        in_specs=placed,
        out_specs=(
            P("lat", "lon", None),
            P("lat", "lon", None),
            P(("lat", "lon"), None, None, None),
        ),
        check_vma=False,
    )
```

```python
import functools
import math

import jax
import jax.numpy as jnp
import numpy as np
from jax import lax
from jax.experimental import pallas as pl
from jax.experimental.pallas import tpu as pltpu
from jax.sharding import PartitionSpec as P

ROWS = 384
COLS = 768
WAVES = 256
CHANNELS = 128
RES = 4096
BLOCK = 128
CONN = 8
TILE = 2
WINDOW = 6
LATS = 8
LONS = 16
DEVICES = LATS * LONS
CHIPS = DEVICES // 2
SUB_ROWS = ROWS // DEVICES
BAND = 48
HALF = 28
SENT_COLS = 2 * HALF
TILES = 24
FRAME = TILES + 2
CHUNK = 1024
CHUNKS = RES // CHUNK
FRAME_ROWS = 736
MB = 1 << 20
MESH = pl.DeviceIdType.MESH
FAR = (2, 1, 1, 0)
SPLIT = (7, 16, 24, 32)
LANES = SUB_ROWS * CHANNELS
NODES = TILES * TILES


def geometry():
    j = np.arange(ROWS).reshape(CHIPS, 2, SUB_ROWS).transpose(2, 1, 0).reshape(-1)
    colatitude = (j + 0.5) * (math.pi / ROWS)
    return np.cos(colatitude), np.sin(colatitude)


def log_terms():
    index = np.arange(WAVES).astype(np.float64)
    return np.where(index > 0, np.log1p(0.5 / np.maximum(index, 1.0)), 0.0)


def forward_rows():
    m = np.arange(WAVES)[:, None]
    k = np.arange(COLS)[None, :]
    angle = (m * k % COLS) * (2.0 * math.pi / COLS)
    table = np.stack([np.cos(angle), -np.sin(angle)], axis=1) / COLS
    return table.reshape(2 * WAVES, COLS)


def inverse_columns():
    o = np.arange(LONS)[:, None, None]
    b = np.arange(2)[None, :, None]
    t = np.arange(HALF)[None, None, :]
    k = ((BAND * o - 2 + 2 * t + b) % COLS).reshape(-1)
    m = np.arange(WAVES)[None, :]
    angle = (m * k[:, None] % COLS) * (2.0 * math.pi / COLS)
    factor = np.where(m == 0, 1.0, 2.0)
    table = np.stack([factor * np.cos(angle), -factor * np.sin(angle)], axis=2)
    return table.reshape(LONS * SENT_COLS, 2 * WAVES)


def split(table):
    high = table.astype(jnp.bfloat16)
    return high, (table - high.astype(np.float32)).astype(jnp.bfloat16)


def chain_kernel(
    slots_ref,
    index_ref,
    fields_ref,
    order_ref,
    forward_high_ref,
    forward_low_ref,
    inverse_ref,
    cos_ref,
    log_sin_ref,
    weight_ref,
    diffusion_ref,
    logs_ref,
    states_hbm,
    blocks_hbm,
    spectral_ref,
    framed_ref,
    halo_ref,
    recur_hbm,
    states_ref,
    blocks_ref,
    recur_ref,
    sent_ref,
    rows_ref,
    chosen_ref,
    table_ref,
    factor_ref,
    legendre_ref,
    weighted_ref,
    plain_ref,
    zonal_ref,
    sibling_ref,
    message_ref,
    owned_ref,
    wide_ref,
    back_ref,
    reply_ref,
    replied_ref,
    mine_ref,
    other_ref,
    inverted_ref,
    samples_ref,
    load_sem,
    store_sem,
    lon_send,
    lon_recv,
    core_send,
    core_recv,
    out_send,
    out_recv,
    back_send,
    back_recv,
    grid_send,
    grid_recv,
    halo_send,
    halo_recv,
):
    a = lax.axis_index("lat")
    o = lax.axis_index("lon")
    core = lax.rem(o, 2)
    chip = a * (LONS // 2) + lax.div(o, 2)
    sibling = (a, o + 1 - 2 * core)

    z_lo, x = lax.div(a, 4), lax.rem(a, 4)
    z_hi, y = lax.div(o, 8), lax.rem(lax.div(o, 2), 4)
    along = (2, 1, 3, 0)
    xs = [lax.rem(x + by, 4) for by in along]
    ys = [lax.rem(y + by, 4) * 2 for by in along]
    lats = [z * 4 + at for at in xs for z in (1 - z_lo, z_lo)]
    sectors = [z * 8 + at for z in (1 - z_hi, z_hi) for at in ys]
    partners = [(i, j) for i in range(LATS) for j in range(LONS // 2)]
    hops = lambda ij: FAR[ij[0] // 2] + FAR[ij[1] % 4] + (1, 0)[ij[0] % 2] + (2, 0)[ij[1] // 4]
    partners = sorted(partners[:-1], key=hops, reverse=True)

    def lon_at(step):
        at = sectors[step // 2]
        return at + (core if step % 2 else 1 - core)

    def chip_at(step):
        i, j = partners[step]
        return lats[i] * (LONS // 2) + lax.div(sectors[j], 2)

    def chip_device(step):
        i, j = partners[step]
        return (lats[i], sectors[j] + core)

    def each(count, action):
        for s in range(count - 1):
            action(s)

    def load_states(b):
        return pltpu.make_async_copy(
            states_hbm.at[:, pl.ds(pl.multiple_of(b * BLOCK, BLOCK), BLOCK)],
            states_ref.at[b],
            load_sem.at[b],
        )

    load_blocks = pltpu.make_async_copy(blocks_hbm, blocks_ref, load_sem.at[RES // BLOCK])

    barrier = pltpu.get_barrier_semaphore()
    each(
        CHIPS,
        lambda s: pl.semaphore_signal(
            barrier, inc=1, device_id=chip_device(s), device_id_type=MESH
        ),
    )
    each(
        LONS,
        lambda s: pl.semaphore_signal(
            barrier, inc=1, device_id=(a, lon_at(s)), device_id_type=MESH
        ),
    )
    load_blocks.start()
    each(RES // BLOCK + 1, lambda b: load_states(b).start())
    halo_ref[...] = jnp.zeros_like(halo_ref)
    for d in range(LONS):
        sent_ref[d] = fields_ref[d * 144 : (d + 1) * 144, :].astype(jnp.bfloat16)
    pl.semaphore_wait(barrier, LONS + CHIPS - 2)

    def row_copy(s):
        return pltpu.make_async_remote_copy(
            src_ref=sent_ref.at[lon_at(s)],
            dst_ref=rows_ref.at[o],
            send_sem=lon_send.at[s],
            recv_sem=lon_recv.at[s],
            device_id=(a, lon_at(s)),
            device_id_type=MESH,
        )

    each(LONS, lambda s: row_copy(s).start())
    rows_ref[o] = sent_ref[o]

    column = lax.broadcasted_iota(jnp.int32, (WAVES, 2 * WAVES), 1)
    slot = 4 * ((column >> 2) & (CHIPS - 1)) + 2 * (column >> 8) + ((column >> 1) & 1)
    moves = jnp.where(lax.broadcasted_iota(jnp.int32, slot.shape, 0) == slot, 1.0, 0.0)
    waves = jnp.broadcast_to(order_ref[...].astype(jnp.float32), (8, WAVES))
    waves = jnp.dot(
        waves.astype(jnp.bfloat16),
        moves.astype(jnp.bfloat16),
        preferred_element_type=jnp.float32,
    ).astype(jnp.int32)
    key = 2 * waves[0:1] + (column[0:1] & 1)
    entry = lax.broadcasted_iota(jnp.int32, (2 * WAVES, 2 * WAVES), 0)
    chosen_ref[...] = jnp.where(entry == key, 1.0, 0.0).astype(jnp.bfloat16)
    for half, source in enumerate((forward_high_ref, forward_low_ref)):
        table_ref[half] = lax.dot_general(
            chosen_ref[...],
            source[...],
            (((0,), (0,)), ((), ())),
            preferred_element_type=jnp.float32,
        ).astype(jnp.bfloat16)

    level = lax.broadcasted_iota(jnp.int32, (WAVES, CHANNELS), 0).astype(jnp.float32)
    cos_col = cos_ref[...]
    poles = []
    for s in range(2):
        m = slots_ref[2 * (a * LONS + o) + s]
        order = m.astype(jnp.float32)
        above = level > order
        order_sq = order * order
        prior = level - 1.0
        factor = jnp.sqrt(
            jnp.where(above, 4.0 * level * level - 1.0, 0.0)
            / jnp.where(above, level * level - order_sq, 1.0)
        )
        factor_ref[s, 0] = factor
        factor_ref[s, 1] = factor * jnp.sqrt(
            jnp.where(above, prior * prior - order_sq, 0.0)
            / jnp.where(level > 1.5, 4.0 * prior * prior - 1.0, 1.0)
        )
        factor_ref[s, 2] = jnp.where(level == order, 1.0, 0.0)
        index = lax.broadcasted_iota(jnp.int32, (1, WAVES), 1)
        logs = jnp.sum(jnp.where(index <= m, logs_ref[...], 0.0), axis=1, keepdims=True)
        poles.append(
            jnp.exp(0.5 * logs + order * log_sin_ref[...] - 0.5 * math.log(2.0))
        )

    def eight(base, carry):
        state = list(carry)
        at = pl.ds(pl.multiple_of(base * 8, 8), 8)
        for s in range(2):
            previous, current = state[s]
            factors = [factor_ref[s, f, at, :] for f in range(3)]
            stacked = []
            for step in range(8):
                row, drop, first = [
                    jnp.concatenate([f[step : step + 1]] * SUB_ROWS, axis=1) for f in factors
                ]
                value = row * (cos_col * current) - drop * previous + first * poles[s]
                previous, current = current, value
                stacked.append(value)
            state[s] = (previous, current)
            legendre_ref[s, at, :] = jnp.concatenate(stacked, axis=0)
        return tuple(state)

    zero = jnp.zeros((1, ROWS), jnp.float32)
    lax.fori_loop(0, WAVES // 8, eight, ((zero, zero), (zero, zero)))
    for s in range(2):
        table = legendre_ref[s]
        plain_ref[s] = table.astype(jnp.bfloat16)
        table = table * weight_ref[...]
        high = table.astype(jnp.bfloat16)
        weighted_ref[0, s] = high
        weighted_ref[1, s] = (table - high.astype(jnp.float32)).astype(jnp.bfloat16)

    def recur_blocks(part, first, last):
        def one(g, carry):
            left = jnp.concatenate(
                [states_ref[index_ref[l, g]] for l in range(CONN)],
                axis=1,
            )
            right = jnp.concatenate([blocks_ref[g, l] for l in range(CONN)], axis=1)
            recur_ref[:, pl.ds(pl.multiple_of(g * BLOCK, BLOCK), BLOCK)] = lax.dot_general(
                left, right, (((1,), (1,)), ((), ())), preferred_element_type=jnp.float32
            ).astype(jnp.bfloat16)
            return carry

        lax.fori_loop(first, last, one, 0)
        columns = pl.ds(first * BLOCK, (last - first) * BLOCK)
        copy = pltpu.make_async_copy(
            recur_ref.at[:, columns], recur_hbm.at[:, columns], store_sem.at[part]
        )
        copy.start()
        return copy

    each(RES // BLOCK + 1, lambda b: load_states(b).wait())
    load_blocks.wait()
    stores = [recur_blocks(0, 0, SPLIT[0])]
    each(LONS, lambda s: row_copy(s).wait_recv())

    data = rows_ref[...].reshape(LONS, SUB_ROWS, BAND, CHANNELS)
    data = jnp.concatenate(
        [data[:, r].reshape(COLS, CHANNELS) for r in range(SUB_ROWS)], axis=1
    )

    def transform(part):
        at = pl.ds(pl.multiple_of(part * WAVES, WAVES), WAVES)
        return jnp.dot(
            table_ref[0, at, :], data, preferred_element_type=jnp.float32
        ) + jnp.dot(table_ref[1, at, :], data, preferred_element_type=jnp.float32)

    zonal_ref[...] = transform(1 - core).astype(jnp.bfloat16)
    to_sibling = pltpu.make_async_remote_copy(
        src_ref=zonal_ref,
        dst_ref=sibling_ref,
        send_sem=core_send.at[0],
        recv_sem=core_recv.at[0],
        device_id=sibling,
        device_id_type=MESH,
    )
    to_sibling.start()
    own = transform(core)
    to_sibling.wait_recv()
    got = sibling_ref[...].astype(jnp.float32)
    lower = jnp.where(core == 0, own, got).reshape(CHIPS, 4, LANES)
    upper = jnp.where(core == 0, got, own).reshape(CHIPS, 4, LANES)
    message_ref[...] = jnp.concatenate([lower, upper], axis=1).astype(jnp.bfloat16)

    def out_copy(s):
        return pltpu.make_async_remote_copy(
            src_ref=message_ref.at[chip_at(s)],
            dst_ref=owned_ref.at[chip],
            send_sem=out_send,
            recv_sem=out_recv,
            device_id=chip_device(s),
            device_id_type=MESH,
        )

    out_all = pltpu.make_async_remote_copy(
        src_ref=message_ref.at[pl.ds(0, CHIPS - 1)],
        dst_ref=owned_ref.at[pl.ds(0, CHIPS - 1)],
        send_sem=out_send,
        recv_sem=out_recv,
        device_id=sibling,
        device_id_type=MESH,
    )
    each(CHIPS, lambda s: out_copy(s).start())
    owned_ref[chip] = message_ref[chip]

    for half in range(2):
        inverted_ref[half] = jnp.dot(
            inverse_ref[...],
            chosen_ref[:, half * WAVES : (half + 1) * WAVES],
            preferred_element_type=jnp.float32,
        ).astype(jnp.bfloat16)
    stores.append(recur_blocks(1, SPLIT[0], SPLIT[1]))
    out_all.wait_recv()

    for r in range(SUB_ROWS):
        wide_ref[r] = (
            owned_ref[:, :, r * 128 : (r + 1) * 128]
            .astype(jnp.float32)
            .reshape(CHIPS * 8, CHANNELS)
        )
    scaled = level * (level + 1.0) / float((WAVES - 1) * WAVES)
    damping = 1.0 / (1.0 + diffusion_ref[...] * (scaled * scaled))
    damping = jnp.concatenate([damping, damping], axis=1)
    for s in range(2):
        zonal = jnp.concatenate(
            [
                jnp.concatenate(
                    [
                        wide_ref[r, pl.ds(4 * h + 2 * s + p, CHIPS, stride=8), :]
                        for r in range(SUB_ROWS)
                        for h in range(2)
                    ],
                    axis=0,
                )
                for p in range(2)
            ],
            axis=1,
        ).astype(jnp.bfloat16)
        filtered = damping * (
            jnp.dot(weighted_ref[0, s], zonal, preferred_element_type=jnp.float32)
            + jnp.dot(weighted_ref[1, s], zonal, preferred_element_type=jnp.float32)
        )
        for p in range(2):
            spectral_ref[s, p] = filtered[:, p * 128 : (p + 1) * 128]
        grid = lax.dot_general(
            plain_ref[s],
            filtered.astype(jnp.bfloat16),
            (((0,), (0,)), ((), ())),
            preferred_element_type=jnp.float32,
        )
        for p in range(2):
            for r in range(SUB_ROWS):
                for h in range(2):
                    at = r * 128 + h * CHIPS
                    back_ref[r, pl.ds(4 * h + 2 * s + p, CHIPS, stride=8), :] = grid[
                        at : at + CHIPS, p * 128 : (p + 1) * 128
                    ]
    for r in range(SUB_ROWS):
        reply_ref[:, :, r * 128 : (r + 1) * 128] = (
            back_ref[r].reshape(CHIPS, 8, CHANNELS).astype(jnp.bfloat16)
        )

    def back_copy(s):
        return pltpu.make_async_remote_copy(
            src_ref=reply_ref.at[chip_at(s)],
            dst_ref=replied_ref.at[chip],
            send_sem=back_send,
            recv_sem=back_recv,
            device_id=chip_device(s),
            device_id_type=MESH,
        )

    back_all = pltpu.make_async_remote_copy(
        src_ref=reply_ref.at[pl.ds(0, CHIPS - 1)],
        dst_ref=replied_ref.at[pl.ds(0, CHIPS - 1)],
        send_sem=back_send,
        recv_sem=back_recv,
        device_id=sibling,
        device_id_type=MESH,
    )
    each(CHIPS, lambda s: back_copy(s).start())
    replied_ref[chip] = reply_ref[chip]
    stores.append(recur_blocks(2, SPLIT[1], SPLIT[2]))
    back_all.wait_recv()

    whole = replied_ref[...].astype(jnp.float32)
    lower = whole[:, 0:4].reshape(2 * CHIPS * 2, LANES)
    upper = whole[:, 4:8].reshape(2 * CHIPS * 2, LANES)
    other_ref[...] = jnp.where(core == 0, upper, lower).astype(jnp.bfloat16)
    for_sibling = pltpu.make_async_remote_copy(
        src_ref=other_ref,
        dst_ref=mine_ref,
        send_sem=core_send.at[1],
        recv_sem=core_recv.at[1],
        device_id=sibling,
        device_id_type=MESH,
    )
    for_sibling.start()
    kept = jnp.where(core == 0, lower, upper).astype(jnp.bfloat16)
    own = jnp.dot(inverted_ref[core], kept, preferred_element_type=jnp.float32)
    for_sibling.wait_recv()
    own += jnp.dot(inverted_ref[1 - core], mine_ref[...], preferred_element_type=jnp.float32)
    for d in range(LONS):
        samples_ref[d] = own[d * SENT_COLS : (d + 1) * SENT_COLS].astype(jnp.bfloat16)

    def grid_copy(s):
        return pltpu.make_async_remote_copy(
            src_ref=samples_ref.at[lon_at(s)],
            dst_ref=framed_ref.at[o],
            send_sem=grid_send.at[s],
            recv_sem=grid_recv.at[o],
            device_id=(a, lon_at(s)),
            device_id_type=MESH,
        )

    def grid_from(source):
        return pltpu.make_async_remote_copy(
            src_ref=samples_ref.at[source],
            dst_ref=framed_ref.at[source],
            send_sem=grid_send.at[LONS - 1],
            recv_sem=grid_recv.at[source],
            device_id=(a, source),
            device_id_type=MESH,
        )

    each(LONS, lambda s: grid_copy(s).start())
    framed_ref[o] = samples_ref[o]
    stores.append(recur_blocks(3, SPLIT[2], SPLIT[3]))
    up = pltpu.make_async_remote_copy(
        src_ref=framed_ref.at[LONS - 1, :, pl.ds(CHANNELS, 2 * CHANNELS)],
        dst_ref=halo_ref.at[0],
        send_sem=halo_send.at[0],
        recv_sem=halo_recv.at[0],
        device_id=(lax.rem(a + 1, LATS), o),
        device_id_type=MESH,
    )
    down = pltpu.make_async_remote_copy(
        src_ref=framed_ref.at[0, :, pl.ds(0, 2 * CHANNELS)],
        dst_ref=halo_ref.at[1],
        send_sem=halo_send.at[1],
        recv_sem=halo_recv.at[1],
        device_id=(lax.rem(a + LATS - 1, LATS), o),
        device_id_type=MESH,
    )

    @pl.when(o < LONS - 1)
    def _():
        grid_from(LONS - 1).wait_recv()

    @pl.when(a < LATS - 1)
    def _():
        up.start()

    @pl.when(o > 0)
    def _():
        grid_from(0).wait_recv()

    @pl.when(a > 0)
    def _():
        down.start()

    def arrived(source, carry):
        @pl.when(source != o)
        def _():
            grid_from(source).wait_recv()

        return carry

    lax.fori_loop(1, LONS - 1, arrived, 0)
    each(LONS, lambda s: row_copy(s).wait_send())
    out_all.wait_send()
    back_all.wait_send()
    each(LONS, lambda s: grid_copy(s).wait_send())
    to_sibling.wait_send()
    for_sibling.wait_send()
    for copy in stores:
        copy.wait()

    @pl.when(a < LATS - 1)
    def _():
        up.wait_send()
        down.wait_recv()

    @pl.when(a > 0)
    def _():
        down.wait_send()
        up.wait_recv()


def reservoir_kernel(
    rows_ref,
    halo_ref,
    recur_ref,
    entry_ref,
    gain_ref,
    bias_ref,
    readout_ref,
    coefficients_ref,
    blend_ref,
    next_ref,
    spectral_ref,
    frame_ref,
    drive_ref,
    total_ref,
):
    chunk = pl.program_id(0)
    spectral_ref[...] = coefficients_ref[...]

    @pl.when(chunk == 0)
    def _():
        def row_of(position):
            if position < 2:
                part = halo_ref[0, :, position * 128 : (position + 1) * 128]
            elif position >= BAND + 2:
                at = position - BAND - 2
                part = halo_ref[1, :, at * 128 : (at + 1) * 128]
            else:
                j = position - 2
                at = j % SUB_ROWS
                part = rows_ref[j // SUB_ROWS, :, at * 128 : (at + 1) * 128]
            return part.astype(jnp.float32)

        for group in range(0, FRAME, 4):
            for a in range(2):
                parts = [row_of(2 * i + a) for i in range(group, min(group + 4, FRAME))]
                for b in range(2):
                    block = [part[b * HALF : (b + 1) * HALF] for part in parts]
                    if len(block) < 4:
                        block.append(jnp.zeros((FRAME_ROWS - FRAME * HALF, CHANNELS), jnp.float32))
                    block = jnp.concatenate(block, axis=0)
                    at = (a * 2 + b) * 128
                    frame_ref[group * HALF : group * HALF + block.shape[0], at : at + 128] = (
                        block.astype(jnp.bfloat16)
                    )
        total_ref[...] = jnp.zeros_like(total_ref)

    index = entry_ref[...]
    place = index >> 7
    row_at = (place * 43) >> 8
    col_at = place - WINDOW * row_at
    key = ((row_at & 1) * 2 + (col_at & 1)) * CHANNELS + (index & (CHANNELS - 1))
    pick = jnp.where(
        lax.broadcasted_iota(jnp.int32, (4 * CHANNELS, CHUNK), 0) == key, 1.0, 0.0
    ).astype(jnp.bfloat16)
    drive = jnp.dot(frame_ref[...], pick, preferred_element_type=jnp.float32)
    for q in range(CHUNK // 128):
        drive_ref[q] = drive[:, q * 128 : (q + 1) * 128]
    for q in range(CHUNK // 128):
        lanes = slice(q * 128, (q + 1) * 128)
        col = jnp.broadcast_to(col_at[:, lanes] >> 1, (TILES, 128))
        row = jnp.broadcast_to(row_at[:, lanes] >> 1, (TILES, 128))
        col_one, col_two = col == 1, col == 2
        row_one, row_two = row == 1, row == 2
        gain = gain_ref[:, lanes]
        bias = bias_ref[:, lanes]

        def shifted(i):
            near, next_one, far = [
                drive_ref[q, i * HALF + k : i * HALF + k + TILES, :] for k in range(3)
            ]
            return jnp.where(col_two, far, jnp.where(col_one, next_one, near))

        kept = [shifted(0), shifted(1)]
        for i in range(0, TILES, 2):
            both = []
            recur = recur_ref[i * TILES : (i + 2) * TILES, lanes].astype(jnp.float32)
            for step in range(2):
                kept.append(shifted(i + step + 2))
                near, next_one, far = kept
                picked = jnp.where(row_two, far, jnp.where(row_one, next_one, near))
                kept = kept[1:]
                part = recur[step * TILES : (step + 1) * TILES]
                both.append(jnp.tanh(part + picked * gain + bias))
            next_ref[i * TILES : (i + 2) * TILES, lanes] = jnp.concatenate(both, axis=0).astype(
                jnp.bfloat16
            )
    total_ref[...] += jnp.dot(next_ref[...], readout_ref[...], preferred_element_type=jnp.float32)

    @pl.when(chunk == CHUNKS - 1)
    def _():
        for a in range(2):
            for b in range(2):
                at = (a * 2 + b) * 128
                forecast = frame_ref[:, at : at + 128].astype(jnp.float32)
                for i in range(TILES):
                    start = (i + 1) * HALF + 1
                    blend_ref[pl.ds((2 * i + a) * BAND + b, TILES, stride=2), :] = (
                        forecast[start : start + TILES]
                        + total_ref[i * TILES : (i + 1) * TILES, at : at + 128]
                    )


def shards(
    fields,
    diffusion,
    wave_slots,
    reservoir_state,
    adjacency_blocks,
    adjacency_index,
    input_index,
    input_gain,
    bias,
    readout,
):
    vmem = pl.BlockSpec(memory_space=pltpu.VMEM)
    smem = pl.BlockSpec(memory_space=pltpu.SMEM)
    hbm = pl.BlockSpec(memory_space=pl.ANY)
    bf16 = functools.partial(pltpu.VMEM, dtype=jnp.bfloat16)
    f32 = functools.partial(pltpu.VMEM, dtype=jnp.float32)

    forward_high, forward_low = split(forward_rows().astype(np.float32))
    cos_col, sin_col = geometry()
    spectral, framed, halo, recur = pl.pallas_call(
        chain_kernel,
        out_shape=(
            jax.ShapeDtypeStruct((2, 2, WAVES, CHANNELS), jnp.float32),
            jax.ShapeDtypeStruct((LONS, SENT_COLS, LANES), jnp.bfloat16),
            jax.ShapeDtypeStruct((2, SENT_COLS, 2 * CHANNELS), jnp.bfloat16),
            jax.ShapeDtypeStruct((NODES, RES), jnp.bfloat16),
        ),
        in_specs=[smem] * 2 + [vmem] * 10 + [hbm] * 2,
        out_specs=(vmem, vmem, vmem, hbm),
        scratch_shapes=[
            bf16((RES // BLOCK, NODES, BLOCK)),
            bf16((RES // BLOCK, CONN, BLOCK, BLOCK)),
            bf16((NODES, RES)),
            bf16((LONS, SUB_ROWS * BAND, CHANNELS)),
            bf16((LONS, SUB_ROWS * BAND, CHANNELS)),
            bf16((2 * WAVES, 2 * WAVES)),
            bf16((2, 2 * WAVES, COLS)),
            f32((2, 3, WAVES, CHANNELS)),
            f32((2, WAVES, ROWS)),
            bf16((2, 2, WAVES, ROWS)),
            bf16((2, WAVES, ROWS)),
            bf16((WAVES, LANES)),
            bf16((WAVES, LANES)),
            bf16((CHIPS, 8, LANES)),
            bf16((CHIPS, 8, LANES)),
            f32((SUB_ROWS, 8 * CHIPS, CHANNELS)),
            f32((SUB_ROWS, 8 * CHIPS, CHANNELS)),
            bf16((CHIPS, 8, LANES)),
            bf16((CHIPS, 8, LANES)),
            bf16((WAVES, LANES)),
            bf16((WAVES, LANES)),
            bf16((2, LONS * SENT_COLS, WAVES)),
            bf16((LONS, SENT_COLS, LANES)),
            pltpu.SemaphoreType.DMA((RES // BLOCK + 1,)),
            pltpu.SemaphoreType.DMA((4,)),
            pltpu.SemaphoreType.DMA((LONS,)),
            pltpu.SemaphoreType.DMA((LONS,)),
            pltpu.SemaphoreType.DMA((2,)),
            pltpu.SemaphoreType.DMA((2,)),
            pltpu.SemaphoreType.DMA,
            pltpu.SemaphoreType.DMA,
            pltpu.SemaphoreType.DMA,
            pltpu.SemaphoreType.DMA,
            pltpu.SemaphoreType.DMA((LONS,)),
            pltpu.SemaphoreType.DMA((LONS,)),
            pltpu.SemaphoreType.DMA((2,)),
            pltpu.SemaphoreType.DMA((2,)),
        ],
        compiler_params=pltpu.CompilerParams(
            collective_id=0, has_side_effects=True, vmem_limit_bytes=56 * MB
        ),
        cost_estimate=pl.CostEstimate(
            flops=2 * NODES * RES * CONN * BLOCK, bytes_accessed=30 * MB, transcendentals=0
        ),
        name="chain",
    )(
        wave_slots,
        adjacency_index.T,
        fields.reshape(BAND * BAND, CHANNELS),
        wave_slots[None, :],
        jnp.asarray(forward_high),
        jnp.asarray(forward_low),
        jnp.asarray(inverse_columns(), jnp.bfloat16),
        jnp.asarray(cos_col[None, :], jnp.float32),
        jnp.asarray(np.log(sin_col)[None, :], jnp.float32),
        jnp.asarray((math.pi / ROWS) * sin_col[None, :], jnp.float32),
        diffusion[None, :],
        jnp.asarray(log_terms()[None, :], jnp.float32),
        reservoir_state.reshape(NODES, RES),
        adjacency_blocks,
    )

    const = lambda *zeros: (lambda c: zeros)
    blended, upcoming, spectral = pl.pallas_call(
        reservoir_kernel,
        grid=(CHUNKS,),
        out_shape=(
            jax.ShapeDtypeStruct((BAND * BAND, CHANNELS), jnp.float32),
            jax.ShapeDtypeStruct((NODES, RES), jnp.bfloat16),
            jax.ShapeDtypeStruct((4 * WAVES, CHANNELS), jnp.float32),
        ),
        in_specs=[
            pl.BlockSpec((LONS, SENT_COLS, LANES), const(0, 0, 0)),
            pl.BlockSpec((2, SENT_COLS, 2 * CHANNELS), const(0, 0, 0)),
            pl.BlockSpec((NODES, CHUNK), lambda c: (0, c)),
            pl.BlockSpec((1, CHUNK), lambda c: (0, c)),
            pl.BlockSpec((1, CHUNK), lambda c: (0, c)),
            pl.BlockSpec((1, CHUNK), lambda c: (0, c)),
            pl.BlockSpec((CHUNK, 4 * CHANNELS), lambda c: (c, 0)),
            pl.BlockSpec((4 * WAVES // CHUNKS, CHANNELS), lambda c: (c, 0)),
        ],
        out_specs=(
            pl.BlockSpec((BAND * BAND, CHANNELS), const(0, 0)),
            pl.BlockSpec((NODES, CHUNK), lambda c: (0, c)),
            pl.BlockSpec((4 * WAVES // CHUNKS, CHANNELS), lambda c: (c, 0)),
        ),
        scratch_shapes=[
            pltpu.VMEM((FRAME_ROWS, 4 * CHANNELS), jnp.bfloat16),
            pltpu.VMEM((CHUNK // 128, FRAME_ROWS, 128), jnp.float32),
            pltpu.VMEM((NODES, 4 * CHANNELS), jnp.float32),
        ],
        compiler_params=pltpu.CompilerParams(vmem_limit_bytes=56 * MB),
        cost_estimate=pl.CostEstimate(
            flops=2 * (FRAME_ROWS + NODES) * RES * 4 * CHANNELS,
            bytes_accessed=24 * MB,
            transcendentals=NODES * RES,
        ),
        name="reservoir",
    )(
        framed,
        halo,
        recur,
        input_index[None, :],
        input_gain[None, :],
        bias[None, :],
        readout,
        spectral.reshape(4 * WAVES, CHANNELS),
    )
    return (
        blended.reshape(BAND, BAND, CHANNELS),
        upcoming.reshape(TILES, TILES, RES),
        spectral.reshape(2, 2, WAVES, CHANNELS),
    )


def solution(mesh):
    placed = (P("lat", "lon", None), P(), P(), P("lat", "lon", None), P(), P(), P(), P(), P(), P())
    return jax.shard_map(
        shards,
        mesh=mesh,
        in_specs=placed,
        out_specs=(
            P("lat", "lon", None),
            P("lat", "lon", None),
            P(("lat", "lon"), None, None, None),
        ),
        check_vma=False,
    )
```

```python
import functools
import math

import jax
import jax.numpy as jnp
import numpy as np
from jax import lax
from jax.experimental import pallas as pl
from jax.experimental.pallas import tpu as pltpu
from jax.sharding import PartitionSpec as P

ROWS = 384
COLS = 768
WAVES = 256
CHANNELS = 128
RES = 4096
BLOCK = 128
CONN = 8
TILE = 2
WINDOW = 6
LATS = 8
LONS = 16
DEVICES = LATS * LONS
CHIPS = DEVICES // 2
SUB_ROWS = ROWS // DEVICES
BAND = 48
HALF = 28
SENT_COLS = 2 * HALF
TILES = 24
FRAME = TILES + 2
CHUNK = 1024
CHUNKS = RES // CHUNK
FRAME_ROWS = 736
MB = 1 << 20
MESH = pl.DeviceIdType.MESH
FAR = (2, 1, 1, 0)
SPLIT = (5, 18, 31, 32)
LANES = SUB_ROWS * CHANNELS
NODES = TILES * TILES


def geometry():
    j = np.arange(ROWS).reshape(CHIPS, 2, SUB_ROWS).transpose(2, 1, 0).reshape(-1)
    colatitude = (j + 0.5) * (math.pi / ROWS)
    return np.cos(colatitude), np.sin(colatitude)


def log_terms():
    index = np.arange(WAVES).astype(np.float64)
    return np.where(index > 0, np.log1p(0.5 / np.maximum(index, 1.0)), 0.0)


def forward_rows():
    m = np.arange(WAVES)[:, None]
    k = np.arange(COLS)[None, :]
    angle = (m * k % COLS) * (2.0 * math.pi / COLS)
    table = np.stack([np.cos(angle), -np.sin(angle)], axis=1) / COLS
    return table.reshape(2 * WAVES, COLS)


def inverse_columns():
    o = np.arange(LONS)[:, None, None]
    b = np.arange(2)[None, :, None]
    t = np.arange(HALF)[None, None, :]
    k = ((BAND * o - 2 + 2 * t + b) % COLS).reshape(-1)
    m = np.arange(WAVES)[None, :]
    angle = (m * k[:, None] % COLS) * (2.0 * math.pi / COLS)
    factor = np.where(m == 0, 1.0, 2.0)
    table = np.stack([factor * np.cos(angle), -factor * np.sin(angle)], axis=2)
    return table.reshape(LONS * SENT_COLS, 2 * WAVES)


def split(table):
    high = table.astype(jnp.bfloat16)
    return high, (table - high.astype(np.float32)).astype(jnp.bfloat16)


def chain_kernel(
    slots_ref,
    index_ref,
    order_ref,
    cos_ref,
    log_sin_ref,
    weight_ref,
    diffusion_ref,
    logs_ref,
    fields_hbm,
    forward_high_hbm,
    forward_low_hbm,
    inverse_hbm,
    states_hbm,
    blocks_hbm,
    spectral_hbm,
    framed_ref,
    halo_ref,
    recur_hbm,
    fields_ref,
    forward_high_ref,
    forward_low_ref,
    inverse_ref,
    spectral_ref,
    states_ref,
    blocks_ref,
    recur_ref,
    sent_ref,
    rows_ref,
    chosen_ref,
    table_ref,
    factor_ref,
    legendre_ref,
    weighted_ref,
    plain_ref,
    zonal_ref,
    sibling_ref,
    message_ref,
    owned_ref,
    wide_ref,
    back_ref,
    reply_ref,
    replied_ref,
    mine_ref,
    other_ref,
    inverted_ref,
    partial_ref,
    samples_ref,
    early_sem,
    load_sem,
    store_sem,
    lon_send,
    lon_recv,
    core_send,
    core_recv,
    out_send,
    out_recv,
    back_send,
    back_recv,
    grid_send,
    grid_recv,
    halo_send,
    halo_recv,
):
    a = lax.axis_index("lat")
    o = lax.axis_index("lon")
    core = lax.rem(o, 2)
    chip = a * (LONS // 2) + lax.div(o, 2)
    sibling = (a, o + 1 - 2 * core)

    z_lo, x = lax.div(a, 4), lax.rem(a, 4)
    z_hi, y = lax.div(o, 8), lax.rem(lax.div(o, 2), 4)
    along = (2, 1, 3, 0)
    xs = [lax.rem(x + by, 4) for by in along]
    ys = [lax.rem(y + by, 4) * 2 for by in along]
    lats = [z * 4 + at for at in xs for z in (1 - z_lo, z_lo)]
    sectors = [z * 8 + at for z in (1 - z_hi, z_hi) for at in ys]
    partners = [(i, j) for i in range(LATS) for j in range(LONS // 2)]
    hops = lambda ij: FAR[ij[0] // 2] + FAR[ij[1] % 4] + (1, 0)[ij[0] % 2] + (2, 0)[ij[1] // 4]
    partners = sorted(partners[:-1], key=hops, reverse=True)

    def lon_at(step):
        at = sectors[step // 2]
        return at + (core if step % 2 else 1 - core)

    def chip_at(step):
        i, j = partners[step]
        return lats[i] * (LONS // 2) + lax.div(sectors[j], 2)

    def chip_device(step):
        i, j = partners[step]
        return (lats[i], sectors[j] + core)

    def each(count, action):
        for s in range(count - 1):
            action(s)

    def load_states(b):
        return pltpu.make_async_copy(
            states_hbm.at[:, pl.ds(pl.multiple_of(b * BLOCK, BLOCK), BLOCK)],
            states_ref.at[b],
            load_sem.at[b],
        )

    load_blocks = pltpu.make_async_copy(blocks_hbm, blocks_ref, load_sem.at[RES // BLOCK])

    load_fields = pltpu.make_async_copy(fields_hbm, fields_ref, early_sem.at[0])
    load_tables = [
        pltpu.make_async_copy(source, target, early_sem.at[at + 1])
        for at, (source, target) in enumerate(
            (
                (forward_high_hbm, forward_high_ref),
                (forward_low_hbm, forward_low_ref),
                (inverse_hbm, inverse_ref),
            )
        )
    ]
    store_spectral = pltpu.make_async_copy(spectral_ref, spectral_hbm, early_sem.at[4])
    load_fields.start()

    barrier = pltpu.get_barrier_semaphore()
    each(
        CHIPS,
        lambda s: pl.semaphore_signal(
            barrier, inc=1, device_id=chip_device(s), device_id_type=MESH
        ),
    )
    for step in range(0, LONS, 2):
        pl.semaphore_signal(
            barrier, inc=1, device_id=(a, lon_at(step)), device_id_type=MESH
        )
    for load in load_tables:
        load.start()
    load_blocks.start()
    each(RES // BLOCK + 1, lambda b: load_states(b).start())
    halo_ref[...] = jnp.zeros_like(halo_ref)
    load_fields.wait()
    for d in range(LONS):
        sent_ref[d] = fields_ref[d * 144 : (d + 1) * 144, :].astype(jnp.bfloat16)
    pl.semaphore_wait(barrier, CHIPS - 1 + LONS // 2)

    def row_copy(s):
        return pltpu.make_async_remote_copy(
            src_ref=sent_ref.at[lon_at(s)],
            dst_ref=rows_ref.at[o],
            send_sem=lon_send.at[s],
            recv_sem=lon_recv.at[s],
            device_id=(a, lon_at(s)),
            device_id_type=MESH,
        )

    each(LONS, lambda s: row_copy(s).start())
    rows_ref[o] = sent_ref[o]

    for load in load_tables:
        load.wait()
    column = lax.broadcasted_iota(jnp.int32, (WAVES, 2 * WAVES), 1)
    slot = 4 * ((column >> 2) & (CHIPS - 1)) + 2 * (column >> 8) + ((column >> 1) & 1)
    moves = jnp.where(lax.broadcasted_iota(jnp.int32, slot.shape, 0) == slot, 1.0, 0.0)
    waves = jnp.broadcast_to(order_ref[...].astype(jnp.float32), (8, WAVES))
    waves = jnp.dot(
        waves.astype(jnp.bfloat16),
        moves.astype(jnp.bfloat16),
        preferred_element_type=jnp.float32,
    ).astype(jnp.int32)
    key = 2 * waves[0:1] + (column[0:1] & 1)
    entry = lax.broadcasted_iota(jnp.int32, (2 * WAVES, 2 * WAVES), 0)
    chosen_ref[...] = jnp.where(entry == key, 1.0, 0.0).astype(jnp.bfloat16)
    for half, source in enumerate((forward_high_ref, forward_low_ref)):
        table_ref[half] = lax.dot_general(
            chosen_ref[...],
            source[...],
            (((0,), (0,)), ((), ())),
            preferred_element_type=jnp.float32,
        ).astype(jnp.bfloat16)

    level = lax.broadcasted_iota(jnp.int32, (WAVES, CHANNELS), 0).astype(jnp.float32)
    cos_col = cos_ref[...]
    poles = []
    for s in range(2):
        m = slots_ref[2 * (a * LONS + o) + s]
        order = m.astype(jnp.float32)
        above = level > order
        order_sq = order * order
        prior = level - 1.0
        factor = jnp.sqrt(
            jnp.where(above, 4.0 * level * level - 1.0, 0.0)
            / jnp.where(above, level * level - order_sq, 1.0)
        )
        factor_ref[s, 0] = factor
        factor_ref[s, 1] = factor * jnp.sqrt(
            jnp.where(above, prior * prior - order_sq, 0.0)
            / jnp.where(level > 1.5, 4.0 * prior * prior - 1.0, 1.0)
        )
        factor_ref[s, 2] = jnp.where(level == order, 1.0, 0.0)
        index = lax.broadcasted_iota(jnp.int32, (1, WAVES), 1)
        logs = jnp.sum(jnp.where(index <= m, logs_ref[...], 0.0), axis=1, keepdims=True)
        poles.append(
            jnp.exp(0.5 * logs + order * log_sin_ref[...] - 0.5 * math.log(2.0))
        )

    def eight(base, carry):
        state = list(carry)
        at = pl.ds(pl.multiple_of(base * 8, 8), 8)
        for s in range(2):
            previous, current = state[s]
            factors = [factor_ref[s, f, at, :] for f in range(3)]
            stacked = []
            for step in range(8):
                row, drop, first = [
                    jnp.concatenate([f[step : step + 1]] * SUB_ROWS, axis=1) for f in factors
                ]
                value = row * (cos_col * current) - drop * previous + first * poles[s]
                previous, current = current, value
                stacked.append(value)
            state[s] = (previous, current)
            legendre_ref[s, at, :] = jnp.concatenate(stacked, axis=0)
        return tuple(state)

    zero = jnp.zeros((1, ROWS), jnp.float32)
    lax.fori_loop(0, WAVES // 8, eight, ((zero, zero), (zero, zero)))
    for s in range(2):
        table = legendre_ref[s]
        turned = table.T
        high = turned.astype(jnp.bfloat16)
        low = (turned - high.astype(jnp.float32)).astype(jnp.bfloat16)
        plain_ref[s] = jnp.concatenate([high, low, high], axis=1)
        table = table * weight_ref[...]
        high = table.astype(jnp.bfloat16)
        weighted_ref[0, s] = high
        weighted_ref[1, s] = (table - high.astype(jnp.float32)).astype(jnp.bfloat16)

    def recur_blocks(part, first, last):
        def one(g, carry):
            left = jnp.concatenate(
                [states_ref[index_ref[l, g]] for l in range(CONN)],
                axis=1,
            )
            right = jnp.concatenate([blocks_ref[g, l] for l in range(CONN)], axis=1)
            recur_ref[:, pl.ds(pl.multiple_of(g * BLOCK, BLOCK), BLOCK)] = lax.dot_general(
                left, right, (((1,), (1,)), ((), ())), preferred_element_type=jnp.float32
            ).astype(jnp.bfloat16)
            return carry

        lax.fori_loop(first, last, one, 0)
        columns = pl.ds(first * BLOCK, (last - first) * BLOCK)
        copy = pltpu.make_async_copy(
            recur_ref.at[:, columns], recur_hbm.at[:, columns], store_sem.at[part]
        )
        copy.start()
        return copy

    each(RES // BLOCK + 1, lambda b: load_states(b).wait())
    load_blocks.wait()
    stores = [recur_blocks(0, 0, SPLIT[0])]
    each(LONS, lambda s: row_copy(s).wait_recv())

    data = rows_ref[...].reshape(LONS, SUB_ROWS, BAND, CHANNELS)
    data = jnp.concatenate(
        [data[:, r].reshape(COLS, CHANNELS) for r in range(SUB_ROWS)], axis=1
    )

    def transform(part):
        at = pl.ds(pl.multiple_of(part * WAVES, WAVES), WAVES)
        return jnp.dot(
            table_ref[0, at, :], data, preferred_element_type=jnp.float32
        ) + jnp.dot(table_ref[1, at, :], data, preferred_element_type=jnp.float32)

    zonal_ref[...] = transform(1 - core).astype(jnp.bfloat16)
    to_sibling = pltpu.make_async_remote_copy(
        src_ref=zonal_ref,
        dst_ref=sibling_ref,
        send_sem=core_send.at[0],
        recv_sem=core_recv.at[0],
        device_id=sibling,
        device_id_type=MESH,
    )
    to_sibling.start()
    own = transform(core)
    to_sibling.wait_recv()
    got = sibling_ref[...].astype(jnp.float32)
    lower = jnp.where(core == 0, own, got).reshape(CHIPS, 4, LANES)
    upper = jnp.where(core == 0, got, own).reshape(CHIPS, 4, LANES)
    message_ref[...] = jnp.concatenate([lower, upper], axis=1).astype(jnp.bfloat16)

    def out_copy(s):
        return pltpu.make_async_remote_copy(
            src_ref=message_ref.at[chip_at(s)],
            dst_ref=owned_ref.at[chip],
            send_sem=out_send,
            recv_sem=out_recv,
            device_id=chip_device(s),
            device_id_type=MESH,
        )

    out_all = pltpu.make_async_remote_copy(
        src_ref=message_ref.at[pl.ds(0, CHIPS - 1)],
        dst_ref=owned_ref.at[pl.ds(0, CHIPS - 1)],
        send_sem=out_send,
        recv_sem=out_recv,
        device_id=sibling,
        device_id_type=MESH,
    )
    each(CHIPS, lambda s: out_copy(s).start())
    owned_ref[chip] = message_ref[chip]

    for half in range(2):
        inverted_ref[half] = jnp.dot(
            inverse_ref[...],
            chosen_ref[:, half * WAVES : (half + 1) * WAVES],
            preferred_element_type=jnp.float32,
        ).astype(jnp.bfloat16)
    stores.append(recur_blocks(1, SPLIT[0], SPLIT[1]))
    out_all.wait_recv()

    for r in range(SUB_ROWS):
        wide_ref[r] = (
            owned_ref[:, :, r * 128 : (r + 1) * 128]
            .astype(jnp.float32)
            .reshape(CHIPS * 8, CHANNELS)
        )
    scaled = level * (level + 1.0) / float((WAVES - 1) * WAVES)
    damping = 1.0 / (1.0 + diffusion_ref[...] * (scaled * scaled))
    damping = jnp.concatenate([damping, damping], axis=1)
    for s in range(2):
        zonal = jnp.concatenate(
            [
                jnp.concatenate(
                    [
                        wide_ref[r, pl.ds(4 * h + 2 * s + p, CHIPS, stride=8), :]
                        for r in range(SUB_ROWS)
                        for h in range(2)
                    ],
                    axis=0,
                )
                for p in range(2)
            ],
            axis=1,
        ).astype(jnp.bfloat16)
        filtered = damping * (
            jnp.dot(weighted_ref[0, s], zonal, preferred_element_type=jnp.float32)
            + jnp.dot(weighted_ref[1, s], zonal, preferred_element_type=jnp.float32)
        )
        for p in range(2):
            spectral_ref[s, p] = filtered[:, p * 128 : (p + 1) * 128]
        high = filtered.astype(jnp.bfloat16)
        low = (filtered - high.astype(jnp.float32)).astype(jnp.bfloat16)
        grid = jnp.dot(
            plain_ref[s],
            jnp.concatenate([high, high, low], axis=0),
            preferred_element_type=jnp.float32,
        )
        for p in range(2):
            for r in range(SUB_ROWS):
                for h in range(2):
                    at = r * 128 + h * CHIPS
                    back_ref[r, pl.ds(4 * h + 2 * s + p, CHIPS, stride=8), :] = grid[
                        at : at + CHIPS, p * 128 : (p + 1) * 128
                    ]
    for r in range(SUB_ROWS):
        reply_ref[:, :, r * 128 : (r + 1) * 128] = (
            back_ref[r].reshape(CHIPS, 8, CHANNELS).astype(jnp.bfloat16)
        )

    def back_copy(s):
        return pltpu.make_async_remote_copy(
            src_ref=reply_ref.at[chip_at(s)],
            dst_ref=replied_ref.at[chip],
            send_sem=back_send,
            recv_sem=back_recv,
            device_id=chip_device(s),
            device_id_type=MESH,
        )

    back_all = pltpu.make_async_remote_copy(
        src_ref=reply_ref.at[pl.ds(0, CHIPS - 1)],
        dst_ref=replied_ref.at[pl.ds(0, CHIPS - 1)],
        send_sem=back_send,
        recv_sem=back_recv,
        device_id=sibling,
        device_id_type=MESH,
    )
    each(CHIPS, lambda s: back_copy(s).start())
    store_spectral.start()
    replied_ref[chip] = reply_ref[chip]
    stores.append(recur_blocks(2, SPLIT[1], SPLIT[2]))
    back_all.wait_recv()

    whole = replied_ref[...].astype(jnp.float32)
    lower = whole[:, 0:4].reshape(2 * CHIPS * 2, LANES)
    upper = whole[:, 4:8].reshape(2 * CHIPS * 2, LANES)
    other_ref[...] = jnp.where(core == 0, upper, lower).astype(jnp.bfloat16)
    for_sibling = pltpu.make_async_remote_copy(
        src_ref=other_ref,
        dst_ref=mine_ref,
        send_sem=core_send.at[1],
        recv_sem=core_recv.at[1],
        device_id=sibling,
        device_id_type=MESH,
    )
    for_sibling.start()
    kept = jnp.where(core == 0, lower, upper).astype(jnp.bfloat16)
    partial = jnp.dot(inverted_ref[core], kept, preferred_element_type=jnp.float32)
    for r in range(SUB_ROWS):
        partial_ref[r] = partial[:, r * 128 : (r + 1) * 128]
    for_sibling.wait_recv()

    def grid_copy(r, s):
        return pltpu.make_async_remote_copy(
            src_ref=samples_ref.at[r, lon_at(s)],
            dst_ref=framed_ref.at[r, o],
            send_sem=grid_send,
            recv_sem=grid_recv.at[r, o],
            device_id=(a, lon_at(s)),
            device_id_type=MESH,
        )

    def grid_from(r, source):
        return pltpu.make_async_remote_copy(
            src_ref=samples_ref.at[r, source],
            dst_ref=framed_ref.at[r, source],
            send_sem=grid_send,
            recv_sem=grid_recv.at[r, source],
            device_id=sibling,
            device_id_type=MESH,
        )

    edge = lax.div(o, LONS // 2)
    for r in (1, 2 * edge, 2 - 2 * edge):
        lanes = pl.ds(pl.multiple_of(r * CHANNELS, CHANNELS), CHANNELS)
        sample = partial_ref[r] + jnp.dot(
            inverted_ref[1 - core], mine_ref[:, lanes], preferred_element_type=jnp.float32
        )
        samples_ref[r] = sample.reshape(LONS, SENT_COLS, CHANNELS).astype(jnp.bfloat16)
        each(LONS, lambda s: grid_copy(r, s).start())
        framed_ref[r, o] = samples_ref[r, o]
    stores.append(recur_blocks(3, SPLIT[2], SPLIT[3]))

    up = pltpu.make_async_remote_copy(
        src_ref=framed_ref.at[pl.ds(1, 2), LONS - 1],
        dst_ref=halo_ref.at[0],
        send_sem=halo_send.at[0],
        recv_sem=halo_recv.at[0],
        device_id=(lax.rem(a + 1, LATS), o),
        device_id_type=MESH,
    )
    down = pltpu.make_async_remote_copy(
        src_ref=framed_ref.at[pl.ds(0, 2), 0],
        dst_ref=halo_ref.at[1],
        send_sem=halo_send.at[1],
        recv_sem=halo_recv.at[1],
        device_id=(lax.rem(a + LATS - 1, LATS), o),
        device_id_type=MESH,
    )

    @pl.when(o < LONS - 1)
    def _():
        grid_from(1, LONS - 1).wait_recv()
        grid_from(2, LONS - 1).wait_recv()

    @pl.when(a < LATS - 1)
    def _():
        up.start()

    @pl.when(o > 0)
    def _():
        grid_from(1, 0).wait_recv()
        grid_from(0, 0).wait_recv()

    @pl.when(a > 0)
    def _():
        down.start()

    @pl.when(o < LONS - 1)
    def _():
        grid_from(0, LONS - 1).wait_recv()

    @pl.when(o > 0)
    def _():
        grid_from(2, 0).wait_recv()

    def arrived(source, carry):
        @pl.when(source != o)
        def _():
            for r in range(SUB_ROWS):
                grid_from(r, source).wait_recv()

        return carry

    lax.fori_loop(1, LONS - 1, arrived, 0)
    grid_all = pltpu.make_async_remote_copy(
        src_ref=samples_ref.at[:, pl.ds(0, LONS - 1)],
        dst_ref=framed_ref.at[:, pl.ds(0, LONS - 1)],
        send_sem=grid_send,
        recv_sem=grid_recv.at[0, 0],
        device_id=sibling,
        device_id_type=MESH,
    )
    each(LONS, lambda s: row_copy(s).wait_send())
    out_all.wait_send()
    back_all.wait_send()
    grid_all.wait_send()
    to_sibling.wait_send()
    for_sibling.wait_send()
    store_spectral.wait()
    for copy in stores:
        copy.wait()

    @pl.when(a < LATS - 1)
    def _():
        up.wait_send()
        down.wait_recv()

    @pl.when(a > 0)
    def _():
        down.wait_send()
        up.wait_recv()


def reservoir_kernel(
    rows_ref,
    halo_ref,
    recur_ref,
    entry_ref,
    gain_ref,
    bias_ref,
    readout_ref,
    coefficients_ref,
    blend_ref,
    next_ref,
    spectral_ref,
    frame_ref,
    drive_ref,
    total_ref,
):
    chunk = pl.program_id(0)
    spectral_ref[...] = coefficients_ref[...]

    @pl.when(chunk == 0)
    def _():
        def row_of(position):
            if position < 2:
                part = halo_ref[0, position]
            elif position >= BAND + 2:
                part = halo_ref[1, position - BAND - 2]
            else:
                part = rows_ref[(position - 2) % SUB_ROWS, (position - 2) // SUB_ROWS]
            return part.astype(jnp.float32)

        for group in range(0, FRAME, 4):
            for a in range(2):
                parts = [row_of(2 * i + a) for i in range(group, min(group + 4, FRAME))]
                for b in range(2):
                    block = [part[b * HALF : (b + 1) * HALF] for part in parts]
                    if len(block) < 4:
                        block.append(jnp.zeros((FRAME_ROWS - FRAME * HALF, CHANNELS), jnp.float32))
                    block = jnp.concatenate(block, axis=0)
                    at = (a * 2 + b) * 128
                    frame_ref[group * HALF : group * HALF + block.shape[0], at : at + 128] = (
                        block.astype(jnp.bfloat16)
                    )
        total_ref[...] = jnp.zeros_like(total_ref)

    index = entry_ref[...]
    place = index >> 7
    row_at = (place * 43) >> 8
    col_at = place - WINDOW * row_at
    key = ((row_at & 1) * 2 + (col_at & 1)) * CHANNELS + (index & (CHANNELS - 1))
    pick = jnp.where(
        lax.broadcasted_iota(jnp.int32, (4 * CHANNELS, CHUNK), 0) == key, 1.0, 0.0
    ).astype(jnp.bfloat16)
    drive = jnp.dot(frame_ref[...], pick, preferred_element_type=jnp.float32)
    for q in range(CHUNK // 128):
        drive_ref[q] = drive[:, q * 128 : (q + 1) * 128]
    for q in range(CHUNK // 128):
        lanes = slice(q * 128, (q + 1) * 128)
        col = jnp.broadcast_to(col_at[:, lanes] >> 1, (TILES, 128))
        row = jnp.broadcast_to(row_at[:, lanes] >> 1, (TILES, 128))
        col_one, col_two = col == 1, col == 2
        row_one, row_two = row == 1, row == 2
        gain = gain_ref[:, lanes]
        bias = bias_ref[:, lanes]

        def shifted(i):
            near, next_one, far = [
                drive_ref[q, i * HALF + k : i * HALF + k + TILES, :] for k in range(3)
            ]
            return jnp.where(col_two, far, jnp.where(col_one, next_one, near))

        kept = [shifted(0), shifted(1)]
        for i in range(0, TILES, 2):
            both = []
            recur = recur_ref[i * TILES : (i + 2) * TILES, lanes].astype(jnp.float32)
            for step in range(2):
                kept.append(shifted(i + step + 2))
                near, next_one, far = kept
                picked = jnp.where(row_two, far, jnp.where(row_one, next_one, near))
                kept = kept[1:]
                part = recur[step * TILES : (step + 1) * TILES]
                both.append(jnp.tanh(part + picked * gain + bias))
            next_ref[i * TILES : (i + 2) * TILES, lanes] = jnp.concatenate(both, axis=0).astype(
                jnp.bfloat16
            )
    total_ref[...] += jnp.dot(next_ref[...], readout_ref[...], preferred_element_type=jnp.float32)

    @pl.when(chunk == CHUNKS - 1)
    def _():
        for a in range(2):
            for b in range(2):
                at = (a * 2 + b) * 128
                forecast = frame_ref[:, at : at + 128].astype(jnp.float32)
                for i in range(TILES):
                    start = (i + 1) * HALF + 1
                    blend_ref[pl.ds((2 * i + a) * BAND + b, TILES, stride=2), :] = (
                        forecast[start : start + TILES]
                        + total_ref[i * TILES : (i + 1) * TILES, at : at + 128]
                    )


def shards(
    fields,
    diffusion,
    wave_slots,
    reservoir_state,
    adjacency_blocks,
    adjacency_index,
    input_index,
    input_gain,
    bias,
    readout,
):
    vmem = pl.BlockSpec(memory_space=pltpu.VMEM)
    smem = pl.BlockSpec(memory_space=pltpu.SMEM)
    hbm = pl.BlockSpec(memory_space=pl.ANY)
    bf16 = functools.partial(pltpu.VMEM, dtype=jnp.bfloat16)
    f32 = functools.partial(pltpu.VMEM, dtype=jnp.float32)

    forward_high, forward_low = split(forward_rows().astype(np.float32))
    cos_col, sin_col = geometry()
    spectral, framed, halo, recur = pl.pallas_call(
        chain_kernel,
        out_shape=(
            jax.ShapeDtypeStruct((2, 2, WAVES, CHANNELS), jnp.float32),
            jax.ShapeDtypeStruct((SUB_ROWS, LONS, SENT_COLS, CHANNELS), jnp.bfloat16),
            jax.ShapeDtypeStruct((2, 2, SENT_COLS, CHANNELS), jnp.bfloat16),
            jax.ShapeDtypeStruct((NODES, RES), jnp.bfloat16),
        ),
        in_specs=[smem] * 2 + [vmem] * 6 + [hbm] * 6,
        out_specs=(hbm, vmem, vmem, hbm),
        scratch_shapes=[
            f32((BAND * BAND, CHANNELS)),
            bf16((2 * WAVES, COLS)),
            bf16((2 * WAVES, COLS)),
            bf16((LONS * SENT_COLS, 2 * WAVES)),
            f32((2, 2, WAVES, CHANNELS)),
            bf16((RES // BLOCK, NODES, BLOCK)),
            bf16((RES // BLOCK, CONN, BLOCK, BLOCK)),
            bf16((NODES, RES)),
            bf16((LONS, SUB_ROWS * BAND, CHANNELS)),
            bf16((LONS, SUB_ROWS * BAND, CHANNELS)),
            bf16((2 * WAVES, 2 * WAVES)),
            bf16((2, 2 * WAVES, COLS)),
            f32((2, 3, WAVES, CHANNELS)),
            f32((2, WAVES, ROWS)),
            bf16((2, 2, WAVES, ROWS)),
            bf16((2, ROWS, 3 * WAVES)),
            bf16((WAVES, LANES)),
            bf16((WAVES, LANES)),
            bf16((CHIPS, 8, LANES)),
            bf16((CHIPS, 8, LANES)),
            f32((SUB_ROWS, 8 * CHIPS, CHANNELS)),
            f32((SUB_ROWS, 8 * CHIPS, CHANNELS)),
            bf16((CHIPS, 8, LANES)),
            bf16((CHIPS, 8, LANES)),
            bf16((WAVES, LANES)),
            bf16((WAVES, LANES)),
            bf16((2, LONS * SENT_COLS, WAVES)),
            f32((SUB_ROWS, LONS * SENT_COLS, CHANNELS)),
            bf16((SUB_ROWS, LONS, SENT_COLS, CHANNELS)),
            pltpu.SemaphoreType.DMA((5,)),
            pltpu.SemaphoreType.DMA((RES // BLOCK + 1,)),
            pltpu.SemaphoreType.DMA((4,)),
            pltpu.SemaphoreType.DMA((LONS,)),
            pltpu.SemaphoreType.DMA((LONS,)),
            pltpu.SemaphoreType.DMA((2,)),
            pltpu.SemaphoreType.DMA((2,)),
            pltpu.SemaphoreType.DMA,
            pltpu.SemaphoreType.DMA,
            pltpu.SemaphoreType.DMA,
            pltpu.SemaphoreType.DMA,
            pltpu.SemaphoreType.DMA,
            pltpu.SemaphoreType.DMA((SUB_ROWS, LONS)),
            pltpu.SemaphoreType.DMA((2,)),
            pltpu.SemaphoreType.DMA((2,)),
        ],
        compiler_params=pltpu.CompilerParams(
            collective_id=0, has_side_effects=True, vmem_limit_bytes=56 * MB
        ),
        cost_estimate=pl.CostEstimate(
            flops=2 * NODES * RES * CONN * BLOCK, bytes_accessed=30 * MB, transcendentals=0
        ),
        name="chain",
    )(
        wave_slots,
        adjacency_index.T,
        wave_slots[None, :],
        jnp.asarray(cos_col[None, :], jnp.float32),
        jnp.asarray(np.log(sin_col)[None, :], jnp.float32),
        jnp.asarray((math.pi / ROWS) * sin_col[None, :], jnp.float32),
        diffusion[None, :],
        jnp.asarray(log_terms()[None, :], jnp.float32),
        fields.reshape(BAND * BAND, CHANNELS),
        jnp.asarray(forward_high),
        jnp.asarray(forward_low),
        jnp.asarray(inverse_columns(), jnp.bfloat16),
        reservoir_state.reshape(NODES, RES),
        adjacency_blocks,
    )

    const = lambda *zeros: (lambda c: zeros)
    blended, upcoming, spectral = pl.pallas_call(
        reservoir_kernel,
        grid=(CHUNKS,),
        out_shape=(
            jax.ShapeDtypeStruct((BAND * BAND, CHANNELS), jnp.float32),
            jax.ShapeDtypeStruct((NODES, RES), jnp.bfloat16),
            jax.ShapeDtypeStruct((4 * WAVES, CHANNELS), jnp.float32),
        ),
        in_specs=[
            pl.BlockSpec((SUB_ROWS, LONS, SENT_COLS, CHANNELS), const(0, 0, 0, 0)),
            pl.BlockSpec((2, 2, SENT_COLS, CHANNELS), const(0, 0, 0, 0)),
            pl.BlockSpec((NODES, CHUNK), lambda c: (0, c)),
            pl.BlockSpec((1, CHUNK), lambda c: (0, c)),
            pl.BlockSpec((1, CHUNK), lambda c: (0, c)),
            pl.BlockSpec((1, CHUNK), lambda c: (0, c)),
            pl.BlockSpec((CHUNK, 4 * CHANNELS), lambda c: (c, 0)),
            pl.BlockSpec((4 * WAVES // CHUNKS, CHANNELS), lambda c: (c, 0)),
        ],
        out_specs=(
            pl.BlockSpec((BAND * BAND, CHANNELS), const(0, 0)),
            pl.BlockSpec((NODES, CHUNK), lambda c: (0, c)),
            pl.BlockSpec((4 * WAVES // CHUNKS, CHANNELS), lambda c: (c, 0)),
        ),
        scratch_shapes=[
            pltpu.VMEM((FRAME_ROWS, 4 * CHANNELS), jnp.bfloat16),
            pltpu.VMEM((CHUNK // 128, FRAME_ROWS, 128), jnp.float32),
            pltpu.VMEM((NODES, 4 * CHANNELS), jnp.float32),
        ],
        compiler_params=pltpu.CompilerParams(vmem_limit_bytes=56 * MB),
        cost_estimate=pl.CostEstimate(
            flops=2 * (FRAME_ROWS + NODES) * RES * 4 * CHANNELS,
            bytes_accessed=24 * MB,
            transcendentals=NODES * RES,
        ),
        name="reservoir",
    )(
        framed,
        halo,
        recur,
        input_index[None, :],
        input_gain[None, :],
        bias[None, :],
        readout,
        spectral.reshape(4 * WAVES, CHANNELS),
    )
    return (
        blended.reshape(BAND, BAND, CHANNELS),
        upcoming.reshape(TILES, TILES, RES),
        spectral.reshape(2, 2, WAVES, CHANNELS),
    )


def solution(mesh):
    placed = (P("lat", "lon", None), P(), P(), P("lat", "lon", None), P(), P(), P(), P(), P(), P())
    return jax.shard_map(
        shards,
        mesh=mesh,
        in_specs=placed,
        out_specs=(
            P("lat", "lon", None),
            P("lat", "lon", None),
            P(("lat", "lon"), None, None, None),
        ),
        check_vma=False,
    )
```

```python
import functools
import math

import jax
import jax.numpy as jnp
import numpy as np
from jax import lax
from jax.experimental import pallas as pl
from jax.experimental.pallas import tpu as pltpu
from jax.sharding import PartitionSpec as P

ROWS = 384
COLS = 768
WAVES = 256
CHANNELS = 128
RES = 4096
BLOCK = 128
CONN = 8
TILE = 2
WINDOW = 6
LATS = 8
LONS = 16
DEVICES = LATS * LONS
CHIPS = DEVICES // 2
SUB_ROWS = ROWS // DEVICES
BAND = 48
HALF = 28
SENT_COLS = 2 * HALF
TILES = 24
FRAME = TILES + 2
CHUNK = 1024
CHUNKS = RES // CHUNK
FRAME_ROWS = 688
MB = 1 << 20
MESH = pl.DeviceIdType.MESH
FAR = (2, 1, 1, 0)
SPLIT = (5, 18, 31, 32)
LANES = SUB_ROWS * CHANNELS
NODES = TILES * TILES


def geometry():
    j = np.arange(ROWS).reshape(CHIPS, 2, SUB_ROWS).transpose(2, 1, 0).reshape(-1)
    colatitude = (j + 0.5) * (math.pi / ROWS)
    return np.cos(colatitude), np.sin(colatitude)


def log_terms():
    index = np.arange(WAVES).astype(np.float64)
    return np.where(index > 0, np.log1p(0.5 / np.maximum(index, 1.0)), 0.0)


def forward_rows():
    m = np.arange(WAVES)[:, None]
    k = np.arange(COLS)[None, :]
    angle = (m * k % COLS) * (2.0 * math.pi / COLS)
    table = np.stack([np.cos(angle), -np.sin(angle)], axis=1) / COLS
    return table.reshape(2 * WAVES, COLS)


def inverse_columns():
    o = np.arange(LONS)[:, None, None]
    b = np.arange(2)[None, :, None]
    t = np.arange(HALF)[None, None, :]
    k = ((BAND * o - 2 + 2 * t + b) % COLS).reshape(-1)
    m = np.arange(WAVES)[None, :]
    angle = (m * k[:, None] % COLS) * (2.0 * math.pi / COLS)
    factor = np.where(m == 0, 1.0, 2.0)
    table = np.stack([factor * np.cos(angle), -factor * np.sin(angle)], axis=2)
    return table.reshape(LONS * SENT_COLS, 2 * WAVES)


def split(table):
    high = table.astype(jnp.bfloat16)
    return high, (table - high.astype(np.float32)).astype(jnp.bfloat16)


def chain_kernel(
    slots_ref,
    index_ref,
    order_ref,
    cos_ref,
    log_sin_ref,
    weight_ref,
    diffusion_ref,
    logs_ref,
    fields_hbm,
    forward_high_hbm,
    forward_low_hbm,
    inverse_hbm,
    states_hbm,
    blocks_hbm,
    spectral_hbm,
    framed_ref,
    halo_ref,
    recur_hbm,
    fields_ref,
    forward_high_ref,
    forward_low_ref,
    inverse_ref,
    spectral_ref,
    states_ref,
    blocks_ref,
    recur_ref,
    sent_ref,
    rows_ref,
    chosen_ref,
    table_ref,
    factor_ref,
    legendre_ref,
    weighted_ref,
    plain_ref,
    zonal_ref,
    sibling_ref,
    message_ref,
    owned_ref,
    wide_ref,
    back_ref,
    reply_ref,
    replied_ref,
    mine_ref,
    other_ref,
    inverted_ref,
    partial_ref,
    samples_ref,
    early_sem,
    load_sem,
    store_sem,
    lon_send,
    lon_recv,
    core_send,
    core_recv,
    out_send,
    out_recv,
    back_send,
    back_recv,
    grid_send,
    grid_recv,
    halo_send,
    halo_recv,
):
    a = lax.axis_index("lat")
    o = lax.axis_index("lon")
    core = lax.rem(o, 2)
    chip = a * (LONS // 2) + lax.div(o, 2)
    sibling = (a, o + 1 - 2 * core)

    z_lo, x = lax.div(a, 4), lax.rem(a, 4)
    z_hi, y = lax.div(o, 8), lax.rem(lax.div(o, 2), 4)
    along = (2, 1, 3, 0)
    xs = [lax.rem(x + by, 4) for by in along]
    ys = [lax.rem(y + by, 4) * 2 for by in along]
    lats = [z * 4 + at for at in xs for z in (1 - z_lo, z_lo)]
    sectors = [z * 8 + at for z in (1 - z_hi, z_hi) for at in ys]
    partners = [(i, j) for i in range(LATS) for j in range(LONS // 2)]
    hops = lambda ij: FAR[ij[0] // 2] + FAR[ij[1] % 4] + (1, 0)[ij[0] % 2] + (2, 0)[ij[1] // 4]
    partners = sorted(partners[:-1], key=hops, reverse=True)

    def lon_at(step):
        at = sectors[step // 2]
        return at + (core if step % 2 else 1 - core)

    def chip_at(step):
        i, j = partners[step]
        return lats[i] * (LONS // 2) + lax.div(sectors[j], 2)

    def chip_device(step):
        i, j = partners[step]
        return (lats[i], sectors[j] + core)

    def each(count, action):
        for s in range(count - 1):
            action(s)

    def load_states(b):
        return pltpu.make_async_copy(
            states_hbm.at[:, pl.ds(pl.multiple_of(b * BLOCK, BLOCK), BLOCK)],
            states_ref.at[b],
            load_sem.at[b],
        )

    load_blocks = pltpu.make_async_copy(blocks_hbm, blocks_ref, load_sem.at[RES // BLOCK])

    load_fields = pltpu.make_async_copy(fields_hbm, fields_ref, early_sem.at[0])
    load_tables = [
        pltpu.make_async_copy(source, target, early_sem.at[at + 1])
        for at, (source, target) in enumerate(
            (
                (forward_high_hbm, forward_high_ref),
                (forward_low_hbm, forward_low_ref),
                (inverse_hbm, inverse_ref),
            )
        )
    ]
    store_spectral = pltpu.make_async_copy(spectral_ref, spectral_hbm, early_sem.at[4])
    load_fields.start()

    barrier = pltpu.get_barrier_semaphore()
    each(
        CHIPS,
        lambda s: pl.semaphore_signal(
            barrier, inc=1, device_id=chip_device(s), device_id_type=MESH
        ),
    )
    for step in range(0, LONS, 2):
        pl.semaphore_signal(
            barrier, inc=1, device_id=(a, lon_at(step)), device_id_type=MESH
        )
    for load in load_tables:
        load.start()
    load_blocks.start()
    each(RES // BLOCK + 1, lambda b: load_states(b).start())
    halo_ref[...] = jnp.zeros_like(halo_ref)
    load_fields.wait()
    for d in range(LONS):
        sent_ref[d] = fields_ref[d * 144 : (d + 1) * 144, :].astype(jnp.bfloat16)
    pl.semaphore_wait(barrier, CHIPS - 1 + LONS // 2)

    def row_copy(s):
        return pltpu.make_async_remote_copy(
            src_ref=sent_ref.at[lon_at(s)],
            dst_ref=rows_ref.at[o],
            send_sem=lon_send.at[s],
            recv_sem=lon_recv.at[s],
            device_id=(a, lon_at(s)),
            device_id_type=MESH,
        )

    each(LONS, lambda s: row_copy(s).start())
    rows_ref[o] = sent_ref[o]

    for load in load_tables:
        load.wait()
    column = lax.broadcasted_iota(jnp.int32, (WAVES, 2 * WAVES), 1)
    slot = 4 * ((column >> 2) & (CHIPS - 1)) + 2 * (column >> 8) + ((column >> 1) & 1)
    moves = jnp.where(lax.broadcasted_iota(jnp.int32, slot.shape, 0) == slot, 1.0, 0.0)
    waves = jnp.broadcast_to(order_ref[...].astype(jnp.float32), (8, WAVES))
    waves = jnp.dot(
        waves.astype(jnp.bfloat16),
        moves.astype(jnp.bfloat16),
        preferred_element_type=jnp.float32,
    ).astype(jnp.int32)
    key = 2 * waves[0:1] + (column[0:1] & 1)
    entry = lax.broadcasted_iota(jnp.int32, (2 * WAVES, 2 * WAVES), 0)
    chosen_ref[...] = jnp.where(entry == key, 1.0, 0.0).astype(jnp.bfloat16)
    for half, source in enumerate((forward_high_ref, forward_low_ref)):
        table_ref[half] = lax.dot_general(
            chosen_ref[...],
            source[...],
            (((0,), (0,)), ((), ())),
            preferred_element_type=jnp.float32,
        ).astype(jnp.bfloat16)

    level = lax.broadcasted_iota(jnp.int32, (WAVES, CHANNELS), 0).astype(jnp.float32)
    cos_col = cos_ref[...]
    poles = []
    for s in range(2):
        m = slots_ref[2 * (a * LONS + o) + s]
        order = m.astype(jnp.float32)
        above = level > order
        order_sq = order * order
        prior = level - 1.0
        factor = jnp.sqrt(
            jnp.where(above, 4.0 * level * level - 1.0, 0.0)
            / jnp.where(above, level * level - order_sq, 1.0)
        )
        factor_ref[s, 0] = factor
        factor_ref[s, 1] = factor * jnp.sqrt(
            jnp.where(above, prior * prior - order_sq, 0.0)
            / jnp.where(level > 1.5, 4.0 * prior * prior - 1.0, 1.0)
        )
        factor_ref[s, 2] = jnp.where(level == order, 1.0, 0.0)
        index = lax.broadcasted_iota(jnp.int32, (1, WAVES), 1)
        logs = jnp.sum(jnp.where(index <= m, logs_ref[...], 0.0), axis=1, keepdims=True)
        poles.append(
            jnp.exp(0.5 * logs + order * log_sin_ref[...] - 0.5 * math.log(2.0))
        )

    def eight(base, carry):
        state = list(carry)
        at = pl.ds(pl.multiple_of(base * 8, 8), 8)
        for s in range(2):
            previous, current = state[s]
            factors = [factor_ref[s, f, at, :] for f in range(3)]
            stacked = []
            for step in range(8):
                row, drop, first = [
                    jnp.concatenate([f[step : step + 1]] * SUB_ROWS, axis=1) for f in factors
                ]
                value = row * (cos_col * current) - drop * previous + first * poles[s]
                previous, current = current, value
                stacked.append(value)
            state[s] = (previous, current)
            legendre_ref[s, at, :] = jnp.concatenate(stacked, axis=0)
        return tuple(state)

    zero = jnp.zeros((1, ROWS), jnp.float32)
    lax.fori_loop(0, WAVES // 8, eight, ((zero, zero), (zero, zero)))
    for s in range(2):
        table = legendre_ref[s]
        turned = table.T
        high = turned.astype(jnp.bfloat16)
        low = (turned - high.astype(jnp.float32)).astype(jnp.bfloat16)
        plain_ref[s] = jnp.concatenate([high, low, high], axis=1)
        table = table * weight_ref[...]
        high = table.astype(jnp.bfloat16)
        weighted_ref[0, s] = high
        weighted_ref[1, s] = (table - high.astype(jnp.float32)).astype(jnp.bfloat16)

    def recur_blocks(part, first, last):
        def one(g, carry):
            left = jnp.concatenate(
                [states_ref[index_ref[l, g]] for l in range(CONN)],
                axis=1,
            )
            right = jnp.concatenate([blocks_ref[g, l] for l in range(CONN)], axis=1)
            recur_ref[:, pl.ds(pl.multiple_of(g * BLOCK, BLOCK), BLOCK)] = lax.dot_general(
                left, right, (((1,), (1,)), ((), ())), preferred_element_type=jnp.float32
            ).astype(jnp.bfloat16)
            return carry

        lax.fori_loop(first, last, one, 0)
        columns = pl.ds(first * BLOCK, (last - first) * BLOCK)
        copy = pltpu.make_async_copy(
            recur_ref.at[:, columns], recur_hbm.at[:, columns], store_sem.at[part]
        )
        copy.start()
        return copy

    each(RES // BLOCK + 1, lambda b: load_states(b).wait())
    load_blocks.wait()
    stores = [recur_blocks(0, 0, SPLIT[0])]
    each(LONS, lambda s: row_copy(s).wait_recv())

    data = rows_ref[...].reshape(LONS, SUB_ROWS, BAND, CHANNELS)
    data = jnp.concatenate(
        [data[:, r].reshape(COLS, CHANNELS) for r in range(SUB_ROWS)], axis=1
    )

    def transform(part):
        at = pl.ds(pl.multiple_of(part * WAVES, WAVES), WAVES)
        return jnp.dot(
            table_ref[0, at, :], data, preferred_element_type=jnp.float32
        ) + jnp.dot(table_ref[1, at, :], data, preferred_element_type=jnp.float32)

    zonal_ref[...] = transform(1 - core).astype(jnp.bfloat16)
    to_sibling = pltpu.make_async_remote_copy(
        src_ref=zonal_ref,
        dst_ref=sibling_ref,
        send_sem=core_send.at[0],
        recv_sem=core_recv.at[0],
        device_id=sibling,
        device_id_type=MESH,
    )
    to_sibling.start()
    own = transform(core)
    to_sibling.wait_recv()
    got = sibling_ref[...].astype(jnp.float32)
    lower = jnp.where(core == 0, own, got).reshape(CHIPS, 4, LANES)
    upper = jnp.where(core == 0, got, own).reshape(CHIPS, 4, LANES)
    message_ref[...] = jnp.concatenate([lower, upper], axis=1).astype(jnp.bfloat16)

    def out_copy(s):
        return pltpu.make_async_remote_copy(
            src_ref=message_ref.at[chip_at(s)],
            dst_ref=owned_ref.at[chip],
            send_sem=out_send,
            recv_sem=out_recv,
            device_id=chip_device(s),
            device_id_type=MESH,
        )

    out_all = pltpu.make_async_remote_copy(
        src_ref=message_ref.at[pl.ds(0, CHIPS - 1)],
        dst_ref=owned_ref.at[pl.ds(0, CHIPS - 1)],
        send_sem=out_send,
        recv_sem=out_recv,
        device_id=sibling,
        device_id_type=MESH,
    )
    each(CHIPS, lambda s: out_copy(s).start())
    owned_ref[chip] = message_ref[chip]

    for half in range(2):
        inverted_ref[half] = jnp.dot(
            inverse_ref[...],
            chosen_ref[:, half * WAVES : (half + 1) * WAVES],
            preferred_element_type=jnp.float32,
        ).astype(jnp.bfloat16)
    stores.append(recur_blocks(1, SPLIT[0], SPLIT[1]))
    out_all.wait_recv()

    for r in range(SUB_ROWS):
        wide_ref[r] = (
            owned_ref[:, :, r * 128 : (r + 1) * 128]
            .astype(jnp.float32)
            .reshape(CHIPS * 8, CHANNELS)
        )
    scaled = level * (level + 1.0) / float((WAVES - 1) * WAVES)
    damping = 1.0 / (1.0 + diffusion_ref[...] * (scaled * scaled))
    damping = jnp.concatenate([damping, damping], axis=1)
    for s in range(2):
        zonal = jnp.concatenate(
            [
                jnp.concatenate(
                    [
                        wide_ref[r, pl.ds(4 * h + 2 * s + p, CHIPS, stride=8), :]
                        for r in range(SUB_ROWS)
                        for h in range(2)
                    ],
                    axis=0,
                )
                for p in range(2)
            ],
            axis=1,
        ).astype(jnp.bfloat16)
        filtered = damping * (
            jnp.dot(weighted_ref[0, s], zonal, preferred_element_type=jnp.float32)
            + jnp.dot(weighted_ref[1, s], zonal, preferred_element_type=jnp.float32)
        )
        for p in range(2):
            spectral_ref[s, p] = filtered[:, p * 128 : (p + 1) * 128]
        high = filtered.astype(jnp.bfloat16)
        low = (filtered - high.astype(jnp.float32)).astype(jnp.bfloat16)
        grid = jnp.dot(
            plain_ref[s],
            jnp.concatenate([high, high, low], axis=0),
            preferred_element_type=jnp.float32,
        )
        for p in range(2):
            for r in range(SUB_ROWS):
                for h in range(2):
                    at = r * 128 + h * CHIPS
                    back_ref[r, pl.ds(4 * h + 2 * s + p, CHIPS, stride=8), :] = grid[
                        at : at + CHIPS, p * 128 : (p + 1) * 128
                    ]
    for r in range(SUB_ROWS):
        reply_ref[:, :, r * 128 : (r + 1) * 128] = (
            back_ref[r].reshape(CHIPS, 8, CHANNELS).astype(jnp.bfloat16)
        )

    def back_copy(s):
        return pltpu.make_async_remote_copy(
            src_ref=reply_ref.at[chip_at(s)],
            dst_ref=replied_ref.at[chip],
            send_sem=back_send,
            recv_sem=back_recv,
            device_id=chip_device(s),
            device_id_type=MESH,
        )

    back_all = pltpu.make_async_remote_copy(
        src_ref=reply_ref.at[pl.ds(0, CHIPS - 1)],
        dst_ref=replied_ref.at[pl.ds(0, CHIPS - 1)],
        send_sem=back_send,
        recv_sem=back_recv,
        device_id=sibling,
        device_id_type=MESH,
    )
    each(CHIPS, lambda s: back_copy(s).start())
    store_spectral.start()
    replied_ref[chip] = reply_ref[chip]
    stores.append(recur_blocks(2, SPLIT[1], SPLIT[2]))
    back_all.wait_recv()

    whole = replied_ref[...].astype(jnp.float32)
    lower = whole[:, 0:4].reshape(2 * CHIPS * 2, LANES)
    upper = whole[:, 4:8].reshape(2 * CHIPS * 2, LANES)
    other_ref[...] = jnp.where(core == 0, upper, lower).astype(jnp.bfloat16)
    for_sibling = pltpu.make_async_remote_copy(
        src_ref=other_ref,
        dst_ref=mine_ref,
        send_sem=core_send.at[1],
        recv_sem=core_recv.at[1],
        device_id=sibling,
        device_id_type=MESH,
    )
    for_sibling.start()
    kept = jnp.where(core == 0, lower, upper).astype(jnp.bfloat16)
    partial = jnp.dot(inverted_ref[core], kept, preferred_element_type=jnp.float32)
    for r in range(SUB_ROWS):
        partial_ref[r] = partial[:, r * 128 : (r + 1) * 128]
    for_sibling.wait_recv()

    def grid_copy(r, s):
        return pltpu.make_async_remote_copy(
            src_ref=samples_ref.at[r, lon_at(s)],
            dst_ref=framed_ref.at[r, o],
            send_sem=grid_send,
            recv_sem=grid_recv.at[r, o],
            device_id=(a, lon_at(s)),
            device_id_type=MESH,
        )

    def grid_from(r, source):
        return pltpu.make_async_remote_copy(
            src_ref=samples_ref.at[r, source],
            dst_ref=framed_ref.at[r, source],
            send_sem=grid_send,
            recv_sem=grid_recv.at[r, source],
            device_id=sibling,
            device_id_type=MESH,
        )

    edge = lax.div(o, LONS // 2)
    for r in (1, 2 * edge, 2 - 2 * edge):
        lanes = pl.ds(pl.multiple_of(r * CHANNELS, CHANNELS), CHANNELS)
        sample = partial_ref[r] + jnp.dot(
            inverted_ref[1 - core], mine_ref[:, lanes], preferred_element_type=jnp.float32
        )
        samples_ref[r] = sample.reshape(LONS, SENT_COLS, CHANNELS).astype(jnp.bfloat16)
        each(LONS, lambda s: grid_copy(r, s).start())
        framed_ref[r, o] = samples_ref[r, o]
    stores.append(recur_blocks(3, SPLIT[2], SPLIT[3]))

    up = pltpu.make_async_remote_copy(
        src_ref=framed_ref.at[pl.ds(1, 2), LONS - 1],
        dst_ref=halo_ref.at[0],
        send_sem=halo_send.at[0],
        recv_sem=halo_recv.at[0],
        device_id=(lax.rem(a + 1, LATS), o),
        device_id_type=MESH,
    )
    down = pltpu.make_async_remote_copy(
        src_ref=framed_ref.at[pl.ds(0, 2), 0],
        dst_ref=halo_ref.at[1],
        send_sem=halo_send.at[1],
        recv_sem=halo_recv.at[1],
        device_id=(lax.rem(a + LATS - 1, LATS), o),
        device_id_type=MESH,
    )

    @pl.when(o < LONS - 1)
    def _():
        grid_from(1, LONS - 1).wait_recv()
        grid_from(2, LONS - 1).wait_recv()

    @pl.when(a < LATS - 1)
    def _():
        up.start()

    @pl.when(o > 0)
    def _():
        grid_from(1, 0).wait_recv()
        grid_from(0, 0).wait_recv()

    @pl.when(a > 0)
    def _():
        down.start()

    @pl.when(o < LONS - 1)
    def _():
        grid_from(0, LONS - 1).wait_recv()

    @pl.when(o > 0)
    def _():
        grid_from(2, 0).wait_recv()

    def arrived(source, carry):
        @pl.when(source != o)
        def _():
            for r in range(SUB_ROWS):
                grid_from(r, source).wait_recv()

        return carry

    lax.fori_loop(1, LONS - 1, arrived, 0)
    grid_all = pltpu.make_async_remote_copy(
        src_ref=samples_ref.at[:, pl.ds(0, LONS - 1)],
        dst_ref=framed_ref.at[:, pl.ds(0, LONS - 1)],
        send_sem=grid_send,
        recv_sem=grid_recv.at[0, 0],
        device_id=sibling,
        device_id_type=MESH,
    )
    each(LONS, lambda s: row_copy(s).wait_send())
    out_all.wait_send()
    back_all.wait_send()
    grid_all.wait_send()
    to_sibling.wait_send()
    for_sibling.wait_send()
    store_spectral.wait()
    for copy in stores:
        copy.wait()

    @pl.when(a < LATS - 1)
    def _():
        up.wait_send()
        down.wait_recv()

    @pl.when(a > 0)
    def _():
        down.wait_send()
        up.wait_recv()


def reservoir_kernel(
    rows_ref,
    halo_ref,
    recur_ref,
    entry_ref,
    gain_ref,
    bias_ref,
    readout_ref,
    coefficients_ref,
    blend_ref,
    next_ref,
    spectral_ref,
    frame_ref,
    drive_ref,
    total_ref,
):
    chunk = pl.program_id(0)
    spectral_ref[...] = coefficients_ref[...]

    @pl.when(chunk == 0)
    def _():
        def row_of(position):
            if position < 2:
                part = halo_ref[0, position]
            elif position >= BAND + 2:
                part = halo_ref[1, position - BAND - 2]
            else:
                part = rows_ref[(position - 2) % SUB_ROWS, (position - 2) // SUB_ROWS]
            return part.astype(jnp.float32)

        for group in range(0, FRAME, 8):
            for a in range(2):
                parts = [row_of(2 * i + a) for i in range(group, min(group + 8, FRAME))]
                for b in range(2):
                    block = [part[b * HALF : b * HALF + FRAME] for part in parts]
                    if len(block) < 8:
                        block.append(jnp.zeros((FRAME_ROWS - FRAME * FRAME, CHANNELS), jnp.float32))
                    block = jnp.concatenate(block, axis=0)
                    at = (a * 2 + b) * 128
                    frame_ref[group * FRAME : group * FRAME + block.shape[0], at : at + 128] = (
                        block.astype(jnp.bfloat16)
                    )
        total_ref[...] = jnp.zeros_like(total_ref)

    index = entry_ref[...]
    place = index >> 7
    row_at = (place * 43) >> 8
    col_at = place - WINDOW * row_at
    key = ((row_at & 1) * 2 + (col_at & 1)) * CHANNELS + (index & (CHANNELS - 1))
    pick = jnp.where(
        lax.broadcasted_iota(jnp.int32, (4 * CHANNELS, CHUNK), 0) == key, 1.0, 0.0
    ).astype(jnp.bfloat16)
    drive = jnp.dot(frame_ref[...], pick, preferred_element_type=jnp.float32)
    for q in range(CHUNK // 128):
        drive_ref[q] = drive[:, q * 128 : (q + 1) * 128]
    for q in range(CHUNK // 128):
        lanes = slice(q * 128, (q + 1) * 128)
        col = jnp.broadcast_to(col_at[:, lanes] >> 1, (TILES, 128))
        row = jnp.broadcast_to(row_at[:, lanes] >> 1, (TILES, 128))
        col_one, col_two = col == 1, col == 2
        row_one, row_two = row == 1, row == 2
        gain = gain_ref[:, lanes]
        bias = bias_ref[:, lanes]

        def shifted(i):
            near, next_one, far = [
                drive_ref[q, i * FRAME + k : i * FRAME + k + TILES, :] for k in range(3)
            ]
            return jnp.where(col_two, far, jnp.where(col_one, next_one, near))

        kept = [shifted(0), shifted(1)]
        for i in range(0, TILES, 2):
            both = []
            recur = recur_ref[i * TILES : (i + 2) * TILES, lanes].astype(jnp.float32)
            for step in range(2):
                kept.append(shifted(i + step + 2))
                near, next_one, far = kept
                picked = jnp.where(row_two, far, jnp.where(row_one, next_one, near))
                kept = kept[1:]
                part = recur[step * TILES : (step + 1) * TILES]
                both.append(jnp.tanh(part + picked * gain + bias))
            next_ref[i * TILES : (i + 2) * TILES, lanes] = jnp.concatenate(both, axis=0).astype(
                jnp.bfloat16
            )
    total_ref[...] += jnp.dot(next_ref[...], readout_ref[...], preferred_element_type=jnp.float32)

    @pl.when(chunk == CHUNKS - 1)
    def _():
        for a in range(2):
            for b in range(2):
                at = (a * 2 + b) * 128
                forecast = frame_ref[:, at : at + 128].astype(jnp.float32)
                for i in range(TILES):
                    start = (i + 1) * FRAME + 1
                    blend_ref[pl.ds((2 * i + a) * BAND + b, TILES, stride=2), :] = (
                        forecast[start : start + TILES]
                        + total_ref[i * TILES : (i + 1) * TILES, at : at + 128]
                    )


def shards(
    fields,
    diffusion,
    wave_slots,
    reservoir_state,
    adjacency_blocks,
    adjacency_index,
    input_index,
    input_gain,
    bias,
    readout,
):
    vmem = pl.BlockSpec(memory_space=pltpu.VMEM)
    smem = pl.BlockSpec(memory_space=pltpu.SMEM)
    hbm = pl.BlockSpec(memory_space=pl.ANY)
    bf16 = functools.partial(pltpu.VMEM, dtype=jnp.bfloat16)
    f32 = functools.partial(pltpu.VMEM, dtype=jnp.float32)

    forward_high, forward_low = split(forward_rows().astype(np.float32))
    cos_col, sin_col = geometry()
    spectral, framed, halo, recur = pl.pallas_call(
        chain_kernel,
        out_shape=(
            jax.ShapeDtypeStruct((2, 2, WAVES, CHANNELS), jnp.float32),
            jax.ShapeDtypeStruct((SUB_ROWS, LONS, SENT_COLS, CHANNELS), jnp.bfloat16),
            jax.ShapeDtypeStruct((2, 2, SENT_COLS, CHANNELS), jnp.bfloat16),
            jax.ShapeDtypeStruct((NODES, RES), jnp.bfloat16),
        ),
        in_specs=[smem] * 2 + [vmem] * 6 + [hbm] * 6,
        out_specs=(hbm, vmem, vmem, hbm),
        scratch_shapes=[
            f32((BAND * BAND, CHANNELS)),
            bf16((2 * WAVES, COLS)),
            bf16((2 * WAVES, COLS)),
            bf16((LONS * SENT_COLS, 2 * WAVES)),
            f32((2, 2, WAVES, CHANNELS)),
            bf16((RES // BLOCK, NODES, BLOCK)),
            bf16((RES // BLOCK, CONN, BLOCK, BLOCK)),
            bf16((NODES, RES)),
            bf16((LONS, SUB_ROWS * BAND, CHANNELS)),
            bf16((LONS, SUB_ROWS * BAND, CHANNELS)),
            bf16((2 * WAVES, 2 * WAVES)),
            bf16((2, 2 * WAVES, COLS)),
            f32((2, 3, WAVES, CHANNELS)),
            f32((2, WAVES, ROWS)),
            bf16((2, 2, WAVES, ROWS)),
            bf16((2, ROWS, 3 * WAVES)),
            bf16((WAVES, LANES)),
            bf16((WAVES, LANES)),
            bf16((CHIPS, 8, LANES)),
            bf16((CHIPS, 8, LANES)),
            f32((SUB_ROWS, 8 * CHIPS, CHANNELS)),
            f32((SUB_ROWS, 8 * CHIPS, CHANNELS)),
            bf16((CHIPS, 8, LANES)),
            bf16((CHIPS, 8, LANES)),
            bf16((WAVES, LANES)),
            bf16((WAVES, LANES)),
            bf16((2, LONS * SENT_COLS, WAVES)),
            f32((SUB_ROWS, LONS * SENT_COLS, CHANNELS)),
            bf16((SUB_ROWS, LONS, SENT_COLS, CHANNELS)),
            pltpu.SemaphoreType.DMA((5,)),
            pltpu.SemaphoreType.DMA((RES // BLOCK + 1,)),
            pltpu.SemaphoreType.DMA((4,)),
            pltpu.SemaphoreType.DMA((LONS,)),
            pltpu.SemaphoreType.DMA((LONS,)),
            pltpu.SemaphoreType.DMA((2,)),
            pltpu.SemaphoreType.DMA((2,)),
            pltpu.SemaphoreType.DMA,
            pltpu.SemaphoreType.DMA,
            pltpu.SemaphoreType.DMA,
            pltpu.SemaphoreType.DMA,
            pltpu.SemaphoreType.DMA,
            pltpu.SemaphoreType.DMA((SUB_ROWS, LONS)),
            pltpu.SemaphoreType.DMA((2,)),
            pltpu.SemaphoreType.DMA((2,)),
        ],
        compiler_params=pltpu.CompilerParams(
            collective_id=0, has_side_effects=True, vmem_limit_bytes=56 * MB
        ),
        cost_estimate=pl.CostEstimate(
            flops=2 * NODES * RES * CONN * BLOCK, bytes_accessed=30 * MB, transcendentals=0
        ),
        name="chain",
    )(
        wave_slots,
        adjacency_index.T,
        wave_slots[None, :],
        jnp.asarray(cos_col[None, :], jnp.float32),
        jnp.asarray(np.log(sin_col)[None, :], jnp.float32),
        jnp.asarray((math.pi / ROWS) * sin_col[None, :], jnp.float32),
        diffusion[None, :],
        jnp.asarray(log_terms()[None, :], jnp.float32),
        fields.reshape(BAND * BAND, CHANNELS),
        jnp.asarray(forward_high),
        jnp.asarray(forward_low),
        jnp.asarray(inverse_columns(), jnp.bfloat16),
        reservoir_state.reshape(NODES, RES),
        adjacency_blocks,
    )

    const = lambda *zeros: (lambda c: zeros)
    blended, upcoming, spectral = pl.pallas_call(
        reservoir_kernel,
        grid=(CHUNKS,),
        out_shape=(
            jax.ShapeDtypeStruct((BAND * BAND, CHANNELS), jnp.float32),
            jax.ShapeDtypeStruct((NODES, RES), jnp.bfloat16),
            jax.ShapeDtypeStruct((4 * WAVES, CHANNELS), jnp.float32),
        ),
        in_specs=[
            pl.BlockSpec((SUB_ROWS, LONS, SENT_COLS, CHANNELS), const(0, 0, 0, 0)),
            pl.BlockSpec((2, 2, SENT_COLS, CHANNELS), const(0, 0, 0, 0)),
            pl.BlockSpec((NODES, CHUNK), lambda c: (0, c)),
            pl.BlockSpec((1, CHUNK), lambda c: (0, c)),
            pl.BlockSpec((1, CHUNK), lambda c: (0, c)),
            pl.BlockSpec((1, CHUNK), lambda c: (0, c)),
            pl.BlockSpec((CHUNK, 4 * CHANNELS), lambda c: (c, 0)),
            pl.BlockSpec((4 * WAVES // CHUNKS, CHANNELS), lambda c: (c, 0)),
        ],
        out_specs=(
            pl.BlockSpec((BAND * BAND, CHANNELS), const(0, 0)),
            pl.BlockSpec((NODES, CHUNK), lambda c: (0, c)),
            pl.BlockSpec((4 * WAVES // CHUNKS, CHANNELS), lambda c: (c, 0)),
        ),
        scratch_shapes=[
            pltpu.VMEM((FRAME_ROWS, 4 * CHANNELS), jnp.bfloat16),
            pltpu.VMEM((CHUNK // 128, FRAME_ROWS, 128), jnp.float32),
            pltpu.VMEM((NODES, 4 * CHANNELS), jnp.float32),
        ],
        compiler_params=pltpu.CompilerParams(vmem_limit_bytes=56 * MB),
        cost_estimate=pl.CostEstimate(
            flops=2 * (FRAME_ROWS + NODES) * RES * 4 * CHANNELS,
            bytes_accessed=24 * MB,
            transcendentals=NODES * RES,
        ),
        name="reservoir",
    )(
        framed,
        halo,
        recur,
        input_index[None, :],
        input_gain[None, :],
        bias[None, :],
        readout,
        spectral.reshape(4 * WAVES, CHANNELS),
    )
    return (
        blended.reshape(BAND, BAND, CHANNELS),
        upcoming.reshape(TILES, TILES, RES),
        spectral.reshape(2, 2, WAVES, CHANNELS),
    )


def solution(mesh):
    placed = (P("lat", "lon", None), P(), P(), P("lat", "lon", None), P(), P(), P(), P(), P(), P())
    return jax.shard_map(
        shards,
        mesh=mesh,
        in_specs=placed,
        out_specs=(
            P("lat", "lon", None),
            P("lat", "lon", None),
            P(("lat", "lon"), None, None, None),
        ),
        check_vma=False,
    )
```
